32 devices in a mesh: groups: 2 (over x), seq: 16 (over z, y, core).
Axes of the slice: x: 2, y: 2, z: 4, core: 2. Of those that a mesh axis runs over, the one named last changes fastest.
Arguments:
- projected: bfloat16 [4096, 3072], P(('groups', 'seq')), parts along dimension 0, may hold values from -6 to 6
- decay_log: bfloat16 [4096, 8], P(('groups', 'seq')), parts along dimension 0, may hold values from -0.7 to 0
- destination: int32 [4096], P(('groups', 'seq')), parts along dimension 0, may hold values from 0 to 2047, as said below
- source: int32 [4096], P(('groups', 'seq')), parts along dimension 0, may hold values from 0 to 2047, as said below
- starts: int32 [4096], P(('groups', 'seq')), parts along dimension 0, may hold values from 0 to 1, as said below
- upstream: bfloat16 [4096, 2048], P(('groups', 'seq')), parts along dimension 0, may hold values from -6 to 6
- out_weight: bfloat16 [1024, 2048], replicated, may hold values from -0.1875 to 0.1875
Outputs:
- grad_projected: bfloat16 [4096, 3072], P(('groups', 'seq')), parts along dimension 0
- grad_weight: bfloat16 [32768, 2048], P(('groups', 'seq')), parts along dimension 0
The draws below stay inside these ranges and needn't reach their ends.
There are 2 independent parts, one for each index of `groups`. The reference program is written for one: setup_inputs(seed, part) draws one part's arguments, and reference() takes and returns one part's arrays. A program takes and returns all parts, laid end to end along the dimension named above; an argument that names none is the same for every part. Nothing has to cross between parts.
Inputs may be any that keep to these rules, and one draw needn't show every extreme that they name: `destination`: each rollout, padded to a whole number of groups of 16 packed rows, is dealt row by row to the owners in turn, starting at a first owner of its own; the i-th row of owner o goes to packed position i * 16 + (o - that rollout's first owner) mod 16. So every position is named once, each owner holds its rows in packed order, and each owner sends exactly 8 rows to each shard. source[destination[o]] = o for every owner row o. `starts`: 1 marks the first packed row of a rollout and the first row of the padding at a rollout's end, if it has any; each rollout with its padding covers a whole number of groups of 16 rows, and its padding fewer than 16 rows.
All inputs are finite; a program needn't handle non-finite values.
Results may differ from the reference program's by a relative error of at most 0.0064.
Values may be sent and summed in bfloat16 or wider, within the bound.
No kernel may reach another device: no remote copies, remote signals or barrier semaphores. Data moves between devices by JAX's collectives and lax.ppermute only.
A program may use at most 320 MiB of HBM per device.

```python
import math
import jax
import jax.numpy as jnp
from jax import lax

D = 2048
HEADS = 8
HEAD = 128
ROWS_DEV = 128
GROUP_TOKENS = 2048
N_SEQ = 16


def rollout_plan(base_key):
    shard_count = GROUP_TOKENS // ROWS_DEV
    unit_count = GROUP_TOKENS // shard_count
    random_subkey_list = jax.random.split(base_key, 5)
    long_units = jax.random.randint(random_subkey_list[0], (), 3 * unit_count // 4, 7 * unit_count // 8 + 1, dtype=jnp.int32)
    rest_units = unit_count - long_units
    cut_units = jax.random.randint(random_subkey_list[1], (), rest_units // 4, rest_units - rest_units // 4 + 1, dtype=jnp.int32)
    units = jnp.stack([long_units, cut_units, rest_units - cut_units]).astype(jnp.int32)
    units = units[jax.random.permutation(random_subkey_list[2], 3)]
    ends = jnp.cumsum(units, dtype=jnp.int32)
    begins = ends - units
    first_owner = jax.random.randint(random_subkey_list[3], (3,), 0, shard_count, dtype=jnp.int32)
    pad_amount = jax.random.randint(random_subkey_list[4], (3,), 0, shard_count, dtype=jnp.int32)
    return (shard_count, begins, ends, first_owner, pad_amount)


def group_turn(group, ends, first_owner):
    which = jnp.sum((group[:, None] >= ends[None, :]).astype(jnp.int32), axis=1)
    choose = which[:, None] == jnp.arange(3, dtype=jnp.int32)[None, :]
    return jnp.sum(jnp.where(choose, first_owner[None, :], 0), axis=1).astype(jnp.int32)


def draw_destination(key, part):
    shard_count, begins, ends, first_owner, pad_amount = rollout_plan(jax.random.fold_in(key, 11))
    rows = jnp.arange(GROUP_TOKENS, dtype=jnp.int32)
    owner = rows // ROWS_DEV
    group = rows % ROWS_DEV
    turn = group_turn(group, ends, first_owner)
    return (group * shard_count + (owner - turn) % shard_count).astype(jnp.int32)


def draw_source(key, part):
    shard_count, begins, ends, first_owner, pad_amount = rollout_plan(jax.random.fold_in(key, 11))
    places = jnp.arange(GROUP_TOKENS, dtype=jnp.int32)
    group = places // shard_count
    offset = places % shard_count
    turn = group_turn(group, ends, first_owner)
    owner = (offset + turn) % shard_count
    return (owner * ROWS_DEV + group).astype(jnp.int32)


def draw_starts(key, part):
    shard_count, begins, ends, first_owner, pad_amount = rollout_plan(jax.random.fold_in(key, 11))
    places = jnp.arange(GROUP_TOKENS, dtype=jnp.int32)
    rollout_first = jnp.any(places[:, None] == (begins * shard_count)[None, :], axis=1)
    pad_first = jnp.any((places[:, None] == (ends * shard_count - pad_amount)[None, :]) & (pad_amount[None, :] > 0), axis=1)
    return (rollout_first | pad_first).astype(jnp.int32)


def draw_decay_log(key, part):
    random_subkey_list = jax.random.split(jax.random.fold_in(key, 37), 6)
    fast_count = HEADS // 2
    head_order = jax.random.permutation(random_subkey_list[0], HEADS)
    fast_heads = head_order < fast_count
    fast_rate = jnp.exp(jax.random.uniform(random_subkey_list[1], (HEADS,), jnp.float32, math.log(1.0 / 50.0), math.log(1.0 / 30.0)))
    slow_rate = jnp.exp(jax.random.uniform(random_subkey_list[2], (HEADS,), jnp.float32, math.log(0.1), math.log(0.6))) / GROUP_TOKENS
    head_rate = jnp.where(fast_heads, fast_rate, slow_rate)
    factor = jnp.exp(jax.random.uniform(random_subkey_list[3], (GROUP_TOKENS, HEADS), jnp.float32, math.log(0.5), math.log(2.0)))
    value_entries = -head_rate[None, :] * factor
    surge_row_list = jax.random.randint(random_subkey_list[4], (2,), 0, GROUP_TOKENS)
    surge_matched = jnp.any(jnp.arange(GROUP_TOKENS)[:, None] == surge_row_list[None, :], axis=1)
    surge_log_decay = jax.random.uniform(random_subkey_list[5], (GROUP_TOKENS, 1), jnp.float32, math.log(0.5), math.log(0.8))
    value_entries = jnp.where(surge_matched[:, None], surge_log_decay, value_entries)
    return value_entries.astype(jnp.bfloat16)


def shard_levels(key, shape, cuts, least, largest):
    factor_of, own = 1.0, jax.random.fold_in(key, 6)
    for axis_at, parts in cuts:
        steps = jnp.exp(jax.random.uniform(jax.random.fold_in(own, axis_at), (parts,), jnp.float32, least / len(cuts), largest / len(cuts)))
        factor_of = factor_of * jnp.repeat(steps, shape[axis_at] // parts).reshape([-1 if axis == axis_at else 1 for axis in range(len(shape))])
    return factor_of


def centred(own_key, extent, spread, most, cuts=(), held_as=jnp.bfloat16):
    result = spread * jax.random.normal(own_key, extent, jnp.float32)
    if cuts:
        result = result * shard_levels(own_key, extent, cuts, -0.22, 0.18)
    return jnp.clip(result, -most, most).astype(held_as)


def setup_inputs(seed: int = 0, part: int = 0) -> dict:
    splits = jax.random.split(jax.random.key(seed), 8)
    own_keys = jax.random.split(jax.random.fold_in(splits[7], part), 8)
    return {
        "projected": centred(own_keys[0], (GROUP_TOKENS, 3 * HEADS * HEAD), 1.0, 6.0, ((0, 16),)),
        "decay_log": draw_decay_log(jax.random.fold_in(jax.random.fold_in(splits[7], part), 71), part),
        "destination": draw_destination(jax.random.fold_in(jax.random.fold_in(splits[7], part), 71), part),
        "source": draw_source(jax.random.fold_in(jax.random.fold_in(splits[7], part), 71), part),
        "starts": draw_starts(jax.random.fold_in(jax.random.fold_in(splits[7], part), 71), part),
        "upstream": centred(own_keys[5], (GROUP_TOKENS, D), 1.0, 6.0, ((0, 16),)),
        "out_weight": centred(splits[6], (HEADS * HEAD, D), (HEADS * HEAD) ** -0.5, 0.1875),
    }


norm_eps = 1e-06
highest = lax.Precision.HIGHEST

def decay_terms(log_decay, begin_flags):
    row_count = log_decay.shape[0]
    segment = jnp.cumsum(begin_flags, dtype=jnp.int32)
    running = jnp.cumsum(log_decay, axis=0).T
    position = jnp.arange(row_count, dtype=jnp.int32)
    same = (segment[:, None] == segment[None, :]) & (position[None, :] <= position[:, None])
    spread_gap = jnp.minimum(running[:, :, None] - running[:, None, :], 0.0)
    decay_mix = jnp.where(same[None, :, :], jnp.exp(spread_gap), 0.0)
    enter_decay = jnp.where(segment[None, :] == 0, jnp.exp(running), 0.0)
    leave_decay = jnp.where(segment[None, :] == segment[-1], jnp.exp(jnp.minimum(running[:, -1:] - running, 0.0)), 0.0)
    return (decay_mix, enter_decay, leave_decay)

def reference(projected, decay_log, destination, source, starts, upstream, out_weight):
    inner_width = HEADS * HEAD
    packed = projected[source]
    log_rows = decay_log[source].astype(jnp.float32)

    def blocks(array):
        return array.reshape((N_SEQ, ROWS_DEV) + array.shape[1:])
    query_rows = blocks(packed[:, :inner_width].reshape(GROUP_TOKENS, HEADS, HEAD))
    key_rows = blocks(packed[:, inner_width:2 * inner_width].reshape(GROUP_TOKENS, HEADS, HEAD))
    value_rows = blocks(packed[:, 2 * inner_width:].reshape(GROUP_TOKENS, HEADS, HEAD))
    log_blocks = blocks(log_rows)
    flag_blocks = blocks(starts)

    def block_weights(query_block, key_block, decay_mix):
        scores = jnp.einsum('ihd,shd->his', query_block.astype(jnp.float32), key_block.astype(jnp.float32))
        return (scores * decay_mix).astype(jnp.bfloat16)

    def forward(carried, block_item):
        query_block, key_block, value_block, log_block, flag_block = block_item
        decay_mix, enter_decay, leave_decay = decay_terms(log_block, flag_block)
        weights = block_weights(query_block, key_block, decay_mix)
        output_block_rows = jnp.einsum('his,she->ihe', weights.astype(jnp.float32), value_block.astype(jnp.float32))
        output_block_rows = output_block_rows + enter_decay.T[:, :, None] * jnp.einsum('ihd,hde->ihe', query_block.astype(jnp.float32), carried, precision=highest)
        local_state = jnp.einsum('shd,she->hde', key_block.astype(jnp.float32) * leave_decay.T[:, :, None], value_block.astype(jnp.float32), precision=highest)
        next_state = enter_decay[:, -1][:, None, None] * carried + local_state
        return (next_state, (output_block_rows, carried))
    zero_state = jnp.zeros((HEADS, HEAD, HEAD), jnp.float32)
    _, (output, entering) = lax.scan(forward, zero_state, (query_rows, key_rows, value_rows, log_blocks, flag_blocks))
    norm_scale = jnp.sqrt(lax.optimization_barrier(jnp.mean(output * output, axis=3, keepdims=True)) + norm_eps)
    normed = output / norm_scale
    normed_low = normed.astype(jnp.bfloat16).reshape(N_SEQ, ROWS_DEV, inner_width)
    upstream_blocks = upstream.reshape(N_SEQ, ROWS_DEV, D)

    def block_grad(pair):
        return jnp.dot(pair[0].T, pair[1], preferred_element_type=jnp.float32).astype(jnp.bfloat16)
    grad_weight = lax.map(block_grad, (normed_low, upstream_blocks)).reshape(N_SEQ * inner_width, D)
    grad_normed = jnp.dot(upstream, out_weight.T, preferred_element_type=jnp.float32)
    grad_normed = grad_normed.reshape(N_SEQ, ROWS_DEV, HEADS, HEAD)
    grad_output = ((grad_normed - normed * lax.optimization_barrier(jnp.mean(grad_normed * normed, axis=3, keepdims=True))) / norm_scale).astype(jnp.bfloat16)

    def backward(carried, block_item):
        query_block, key_block, value_block, log_block, flag_block, grad_block, state_block = block_item
        decay_mix, enter_decay, leave_decay = decay_terms(log_block, flag_block)
        weights = block_weights(query_block, key_block, decay_mix)
        query_wide = query_block.astype(jnp.float32)
        key_wide = key_block.astype(jnp.float32)
        value_wide = value_block.astype(jnp.float32)
        grad_wide = grad_block.astype(jnp.float32)
        grad_mix = (jnp.einsum('ihe,she->his', grad_wide, value_wide) * decay_mix).astype(jnp.bfloat16)
        grad_query = jnp.einsum('his,shd->ihd', grad_mix.astype(jnp.float32), key_wide)
        grad_query = grad_query + enter_decay.T[:, :, None] * jnp.einsum('ihe,hde->ihd', grad_wide, state_block, precision=highest)
        grad_key = jnp.einsum('his,ihd->shd', grad_mix.astype(jnp.float32), query_wide)
        grad_key = grad_key + leave_decay.T[:, :, None] * jnp.einsum('hde,she->shd', carried, value_wide, precision=highest)
        grad_value = jnp.einsum('his,ihe->she', weights.astype(jnp.float32), grad_wide)
        grad_value = grad_value + leave_decay.T[:, :, None] * jnp.einsum('hde,shd->she', carried, key_wide, precision=highest)
        local_state = jnp.einsum('thd,the->hde', query_wide * enter_decay.T[:, :, None], grad_wide, precision=highest)
        next_state = enter_decay[:, -1][:, None, None] * carried + local_state
        return (next_state, (grad_query, grad_key, grad_value))
    _, (grad_query, grad_key, grad_value) = lax.scan(backward, zero_state, (query_rows, key_rows, value_rows, log_blocks, flag_blocks, grad_output, entering), reverse=True)
    grad_packed = jnp.concatenate([grad_query.reshape(GROUP_TOKENS, inner_width), grad_key.reshape(GROUP_TOKENS, inner_width), grad_value.reshape(GROUP_TOKENS, inner_width)], axis=1).astype(jnp.bfloat16)
    grad_projected = grad_packed[destination]
    return (grad_projected, grad_weight)
```

```python
import functools

import jax
import jax.numpy as jnp
from jax import lax
from jax.experimental import pallas as pl
from jax.experimental.pallas import tpu as pltpu
from jax.sharding import PartitionSpec as P

norm_eps = 1e-06
LANES = 128
CHUNK = 256
META = 8
bf16 = jnp.bfloat16
f32 = jnp.float32

VMEM = pl.BlockSpec(memory_space=pltpu.VMEM)
SMEM = pl.BlockSpec(memory_space=pltpu.SMEM)
PARAMS = pltpu.CompilerParams(vmem_limit_bytes=48 * 1024 * 1024)


def dot(a, b):
    return lax.dot_general(a, b, (((1,), (0,)), ((), ())), preferred_element_type=f32)


def dot_nt(a, b):
    return lax.dot_general(a, b, (((1,), (1,)), ((), ())), preferred_element_type=f32)


def dot_tn(a, b):
    return lax.dot_general(a, b, (((0,), (0,)), ((), ())), preferred_element_type=f32)


def halves(value):
    high = value.astype(bf16)
    return high, (value - high.astype(f32)).astype(bf16)


def wide(value):
    return jnp.concatenate([value] * (CHUNK // LANES), axis=1)


def iota(shape, dim):
    return lax.broadcasted_iota(jnp.int32, shape, dim)


def call(body, outs, ins, flops=0, moved=0, **more):
    return pl.pallas_call(
        body,
        out_shape=outs,
        compiler_params=PARAMS,
        cost_estimate=pl.CostEstimate(flops=flops, bytes_accessed=moved, transcendentals=0),
        **more,
    )(*ins)


def pack_kernel(heads, segments, rows_ref, decay_ref, starts_ref, out_ref):
    per = rows_ref.shape[0] // segments
    inner = heads * LANES
    eye = jnp.where(iota((LANES, LANES), 0) == iota((LANES, LANES), 1), 1.0, 0.0).astype(bf16)
    decay_rows = dot_tn(decay_ref[...], eye)
    flags = starts_ref[...].astype(f32)
    line = iota((META, LANES), 0)
    for head in range(heads):
        meta = jnp.where(line == 0, decay_rows[head : head + 1, :], jnp.where(line == 1, flags, 0.0))
        for segment in range(segments):
            to = segment * heads + head
            for part in range(3):
                at = part * inner + head * LANES
                out_ref[to, part * per : (part + 1) * per, :] = rows_ref[
                    segment * per : (segment + 1) * per, at : at + LANES
                ]
            out_ref[to, 3 * per :, :] = meta.astype(bf16)


def pack(projected, decay_log, starts, heads, segments):
    rows = projected.shape[0]
    per = rows // segments
    peers = heads * segments
    if per % 16 == 0:
        return call(
            functools.partial(pack_kernel, heads, segments),
            jax.ShapeDtypeStruct((peers, 3 * per + META, LANES), bf16),
            (projected, decay_log, starts.reshape(1, rows)),
            moved=4 * projected.size,
            in_specs=[VMEM] * 3,
            out_specs=VMEM,
        )
    body = projected.reshape(segments, per, 3, heads, LANES).transpose(0, 3, 2, 1, 4)
    body = body.reshape(peers, 3 * per, LANES)
    flags = jnp.broadcast_to(starts.astype(bf16)[None, None, :], (heads, 1, rows))
    meta = jnp.concatenate(
        [decay_log.T[:, None, :], flags, jnp.zeros((heads, META - 2, rows), bf16)], axis=1
    )
    meta = jnp.broadcast_to(meta[None], (segments, heads, META, LANES)).reshape(peers, META, LANES)
    return jnp.concatenate([body, meta], axis=1)


def unpack_kernel(heads, segments, in_ref, out_ref):
    per = out_ref.shape[0] // segments
    inner = heads * LANES
    for segment in range(segments):
        for head in range(heads):
            for part in range(3):
                at = part * inner + head * LANES
                out_ref[segment * per : (segment + 1) * per, at : at + LANES] = in_ref[
                    segment * heads + head, part * per : (part + 1) * per, :
                ]


def unpack(arrived, rows, heads, segments):
    per = rows // segments
    if per % 16 == 0:
        return call(
            functools.partial(unpack_kernel, heads, segments),
            jax.ShapeDtypeStruct((rows, 3 * heads * LANES), bf16),
            (arrived,),
            moved=4 * arrived.size,
            in_specs=[VMEM],
            out_specs=VMEM,
        )
    body = arrived.reshape(segments, heads, 3, per, LANES).transpose(0, 3, 2, 1, 4)
    return body.reshape(rows, 3 * heads * LANES)


def grad_normed_kernel(up_ref, order_ref, weight_ref, out_ref, turned_ref):
    @pl.when(pl.program_id(0) == 0)
    def _():
        rows = up_ref.shape[0]
        pick = iota((rows, rows), 1).astype(f32) == order_ref[...]
        turned_ref[...] = dot(jnp.where(pick, 1.0, 0.0).astype(bf16), up_ref[...]).astype(bf16)

    out_ref[0] = dot_nt(turned_ref[...], weight_ref[...])


def grad_normed_of(upstream, order, out_weight, heads):
    rows, width = upstream.shape
    return call(
        grad_normed_kernel,
        (
            jax.ShapeDtypeStruct((heads, rows, LANES), f32),
            jax.ShapeDtypeStruct((rows, width), bf16),
        ),
        (upstream, order, out_weight),
        flops=2 * rows * out_weight.size,
        moved=2 * (2 * upstream.size + out_weight.size),
        grid=(heads,),
        in_specs=[
            pl.BlockSpec((rows, width), lambda i: (0, 0)),
            pl.BlockSpec((rows, LANES), lambda i: (0, 0)),
            pl.BlockSpec((LANES, width), lambda i: (i, 0)),
        ],
        out_specs=[
            pl.BlockSpec((1, rows, LANES), lambda i: (i, 0, 0)),
            pl.BlockSpec((rows, width), lambda i: (0, 0)),
        ],
    )


def grad_weight_kernel(normed_ref, up_ref, out_ref):
    out_ref[...] = dot_tn(normed_ref[0], up_ref[...]).astype(bf16)


def grad_weight_of(normed, upstream):
    heads, rows, _ = normed.shape
    width = upstream.shape[1]
    return call(
        grad_weight_kernel,
        jax.ShapeDtypeStruct((heads * LANES, width), bf16),
        (normed, upstream),
        flops=2 * rows * heads * LANES * width,
        moved=2 * (upstream.size + normed.size + heads * LANES * width),
        grid=(heads,),
        in_specs=[
            pl.BlockSpec((1, rows, LANES), lambda i: (i, 0, 0)),
            pl.BlockSpec((rows, width), lambda i: (0, 0)),
        ],
        out_specs=pl.BlockSpec((LANES, width), lambda i: (i, 0)),
    )


def part_rows(ref, part, chunk):
    per = ref.shape[1] // 3
    if ref.shape[1] % 16:
        per = (ref.shape[1] - META) // 3
    at = part * per + chunk * 16
    return ref[:, at : at + 16, :].reshape(CHUNK, LANES)


def masks(column_ref, line_ref, chunk):
    column = wide(column_ref[chunk])
    line = line_ref[chunk, 0:1, :]
    return column, line


def forward_kernel(
    chunks, per_seg, where_ref, rows_ref, meta_ref, column_ref, line_ref,
    mix_ref, weights_ref, enter_ref, leave_ref, inner_ref, before_ref, state_ref, last_ref, gains_ref,
):
    owners = meta_ref.shape[0]
    per = CHUNK // owners
    segment = where_ref[0]
    first_block = where_ref[1]
    group = CHUNK // LANES
    meta = meta_ref[...].astype(f32).reshape(owners * META, LANES).astype(bf16)
    row = iota((CHUNK, owners * META), 0)
    pick = jnp.where(iota((CHUNK, owners * META), 1) == (row // per) * META, 1.0, 0.0).astype(bf16)
    all_decay = dot(pick, meta)
    lane = iota((CHUNK, LANES), 1)
    slot = iota((CHUNK, LANES), 0) % per
    ones = jnp.ones((LANES, LANES), bf16)
    place = iota((CHUNK, CHUNK), 1).astype(f32)
    state = jnp.zeros((LANES, LANES), f32)
    before = jnp.ones((1, LANES), f32)
    for chunk in range(chunks):
        column, line = masks(column_ref, line_ref, chunk)
        order = line <= column
        chosen = lane == segment * per_seg + chunk * per + slot
        decay = dot(jnp.where(chosen, all_decay, 0.0).astype(bf16), ones).astype(bf16)
        running = dot(jnp.where(order, 1.0, 0.0).astype(bf16), decay)
        flags = jnp.concatenate(
            [
                meta_ref[first_block + chunk * group + i].astype(f32)[1:2, :]
                for i in range(group)
            ],
            axis=1,
        )
        flags = jnp.broadcast_to(flags, (LANES, CHUNK)).astype(bf16)
        count = dot_nt(jnp.where(place <= column, 1.0, 0.0).astype(bf16), flags)
        turned = jnp.where(lane == 0, running, count).T
        gap = jnp.minimum(wide(running) - turned[0:1, :], 0.0)
        same = order & (wide(count) == turned[1:2, :])
        mix = jnp.where(same, jnp.exp(gap), 0.0)
        last_run = jnp.min(running, axis=0, keepdims=True)
        last_count = jnp.max(count, axis=0, keepdims=True)
        enter = jnp.where(count == 0.0, jnp.exp(running), 0.0)
        leave = jnp.where(
            count == last_count, jnp.exp(jnp.minimum(last_run - running, 0.0)), 0.0
        )
        total = jnp.where(last_count == 0.0, jnp.exp(last_run), 0.0)
        query, key, value = (part_rows(rows_ref, part, chunk) for part in range(3))
        weights = (dot_nt(query, key) * mix).astype(bf16)
        high, low = halves(key.astype(f32) * leave)
        local = dot_tn(high, value) + dot_tn(low, value)
        mix_ref[chunk] = mix
        weights_ref[chunk] = weights
        enter_ref[chunk] = enter
        leave_ref[chunk] = leave
        inner_ref[chunk] = dot(weights, value)
        gains_ref[chunk] = jnp.broadcast_to(total, (8, LANES))
        before_ref[chunk] = jnp.broadcast_to(before, (8, LANES))
        state_ref[chunk] = state
        state = total * state + local
        before = total * before
    last_ref[...] = state
    before_ref[chunks] = jnp.broadcast_to(before, (8, LANES))


def middle_kernel(
    chunks, runs, rows_ref, mix_ref, weights_ref, enter_ref, inner_ref, before_ref,
    state_ref, gains_ref, came_ref, normal_ref,
    normed_ref, query_ref, key_ref, value_ref, back_ref, after_ref, last_ref,
):
    group = CHUNK // LANES
    back = jnp.zeros((LANES, LANES), f32)
    after = jnp.ones((1, LANES), f32)
    came = came_ref[...]
    for chunk in reversed(range(chunks)):
        query, key, value = (part_rows(rows_ref, part, chunk) for part in range(3))
        enter = enter_ref[chunk]
        mix = mix_ref[chunk]
        high, low = halves(state_ref[chunk] + before_ref[chunk, 0:1, :] * came)
        output = inner_ref[chunk] + enter * (dot(query, high) + dot(query, low))
        scale = lax.rsqrt(jnp.mean(output * output, axis=1, keepdims=True) + norm_eps)
        normed = output * scale
        split = normed.reshape(runs, group, CHUNK // (runs * group), LANES)
        for i in range(group):
            normed_ref[chunk * group + i] = split[:, i].reshape(LANES, LANES).astype(bf16)
        normal = jnp.concatenate(
            [
                normal_ref[chunk * group + i].reshape(runs, 1, CHUNK // (runs * group), LANES)
                for i in range(group)
            ],
            axis=1,
        ).reshape(CHUNK, LANES)
        grad = (
            (normal - normed * jnp.mean(normal * normed, axis=1, keepdims=True)) * scale
        ).astype(bf16)
        grad_mix = (dot_nt(grad, value) * mix).astype(bf16)
        grad_query = dot(grad_mix, key) + enter * (dot_nt(grad, high) + dot_nt(grad, low))
        query_ref[:, chunk * 16 : (chunk + 1) * 16, :] = (
            grad_query.astype(bf16).reshape(16, 16, LANES)
        )
        key_ref[chunk] = dot_tn(grad_mix, query)
        value_ref[chunk] = dot_tn(weights_ref[chunk], grad)
        high, low = halves(query.astype(f32) * enter)
        local = dot_tn(high, grad) + dot_tn(low, grad)
        back_ref[chunk] = back
        after_ref[chunk] = jnp.broadcast_to(after, (8, LANES))
        gain = gains_ref[chunk, 0:1, :]
        back = gain * back + local
        after = gain * after
    last_ref[...] = back


def backward_kernel(
    chunks, rows_ref, leave_ref, query_ref, key_ref, value_ref, back_ref, after_ref, came_ref, out_ref
):
    per = chunks * 16
    came = came_ref[...]
    out_ref[:, 0:per, :] = query_ref[...]
    for chunk in range(chunks):
        key, value = (part_rows(rows_ref, part, chunk) for part in (1, 2))
        leave = leave_ref[chunk]
        high, low = halves(back_ref[chunk] + after_ref[chunk, 0:1, :] * came)
        grad_key = key_ref[chunk] + leave * (dot_nt(value, high) + dot_nt(value, low))
        grad_value = value_ref[chunk] + leave * (dot(key, high) + dot(key, low))
        for part, grad in ((1, grad_key), (2, grad_value)):
            at = part * per + chunk * 16
            out_ref[:, at : at + 16, :] = grad.astype(bf16).reshape(16, 16, LANES)


def carried(last, gain, segments, heads, step):
    def shift(value, by):
        pairs = [
            (s * heads + h, (s + by * step) * heads + h)
            for s in range(segments)
            for h in range(heads)
            if 0 <= s + by * step < segments
        ]
        return lax.ppermute(value, "seq", pairs)

    state = shift(last, 1)
    if segments > 2:
        gain = shift(gain, 1)
        by = 1
        while by < segments - 1:
            state, gain = state + gain[0:1, :] * shift(state, by), gain * shift(gain, by)
            by *= 2
    return state


def shards(projected, decay_log, destination, source, starts, upstream, out_weight):
    rows = projected.shape[0]
    heads = decay_log.shape[1]
    peers = lax.axis_size("seq")
    segments = peers // heads
    per_seg = rows // segments
    chunks = heads * rows // CHUNK
    per = CHUNK // peers
    me = lax.axis_index("seq")
    segment = me // heads
    groups = [[s * heads + h for h in range(heads)] for s in range(segments)]

    mine = lax.dynamic_slice(destination, (segment * per_seg,), (per_seg,)).reshape(chunks, 1, per)
    owner = jnp.arange(peers, dtype=jnp.int32).reshape(1, peers, 1)
    spot = jnp.arange(per, dtype=jnp.int32).reshape(1, 1, per)
    position = spot * peers + (owner - me + mine) % peers
    position = position.reshape(chunks, CHUNK).astype(f32)
    column = jnp.broadcast_to(position[:, :, None], (chunks, CHUNK, LANES))
    line = jnp.broadcast_to(position[:, None, :], (chunks, 8, CHUNK))
    capacity = rows // peers
    mine = lax.dynamic_slice(destination, (me * capacity,), (capacity,)).reshape(1, capacity)
    spot = jnp.arange(capacity, dtype=jnp.int32).reshape(1, capacity)
    order = spot * peers + (owner[0] - me + mine) % peers
    order = jnp.broadcast_to(order.reshape(rows, 1).astype(f32), (rows, LANES))
    where = jnp.stack([segment, segment * heads]).astype(jnp.int32)

    def exchange(value):
        return lax.all_to_all(value, "seq", split_axis=0, concat_axis=0, tiled=True)

    arrived = exchange(pack(projected, decay_log, starts, heads, segments))
    normal, turned = grad_normed_of(upstream, order, out_weight, heads)
    meta = arrived[:, 3 * per_seg :, :]
    if per != 16:
        arrived = arrived[:, : 3 * per_seg, :].reshape(peers, 3, chunks, per, LANES)
        arrived = arrived.transpose(1, 2, 0, 3, 4).reshape(3, chunks, 16, 16, LANES)
        arrived = arrived.transpose(2, 0, 1, 3, 4).reshape(16, 3 * chunks * 16, LANES)

    def shape(*dims, dtype=f32):
        return jax.ShapeDtypeStruct(dims, dtype)

    tall = (chunks, CHUNK, LANES)
    square = (chunks, CHUNK, CHUNK)
    small = (chunks, 8, LANES)
    states = (chunks, LANES, LANES)
    mix, weights, enter, leave, inner, before, state, last, gains = call(
        functools.partial(forward_kernel, chunks, per_seg),
        (
            shape(*square), shape(*square, dtype=bf16), shape(*tall), shape(*tall), shape(*tall),
            shape(chunks + 1, 8, LANES), shape(*states), shape(LANES, LANES), shape(*small),
        ),
        (where, arrived, meta, column, line),
        flops=2 * chunks * CHUNK * LANES * 1024,
        moved=2 * arrived.size + 8 * chunks * CHUNK * CHUNK,
        in_specs=[SMEM] + [VMEM] * 4,
        out_specs=[VMEM] * 9,
    )
    came = carried(last, before[chunks], segments, heads, 1)
    normal = lax.all_to_all(
        normal, "seq", split_axis=0, concat_axis=0, tiled=True, axis_index_groups=groups
    )
    runs = peers if per == 16 else 1
    if per != 16:
        normal = normal.reshape(chunks, CHUNK // rows, peers, capacity, LANES)
        normal = normal.swapaxes(1, 2).reshape(heads, rows, LANES)
    normed, grad_query, grad_key, grad_value, back, after, last = call(
        functools.partial(middle_kernel, chunks, runs),
        (
            shape(heads, rows, LANES, dtype=bf16), shape(16, chunks * 16, LANES, dtype=bf16),
            shape(*tall), shape(*tall), shape(*states), shape(*small), shape(LANES, LANES),
        ),
        (arrived, mix, weights, enter, inner, before, state, gains, came, normal),
        flops=2 * chunks * CHUNK * LANES * 2048,
        moved=2 * arrived.size + 8 * chunks * CHUNK * CHUNK,
        in_specs=[VMEM] * 10,
        out_specs=[VMEM] * 7,
    )
    came = carried(last, before[chunks], segments, heads, -1)
    if per != 16:
        normed = normed.reshape(chunks, peers, CHUNK // rows, capacity, LANES)
        normed = normed.swapaxes(1, 2).reshape(heads, rows, LANES)
    normed = lax.all_to_all(
        normed, "seq", split_axis=0, concat_axis=0, tiled=True, axis_index_groups=groups
    )
    grads = call(
        functools.partial(backward_kernel, chunks),
        shape(16, 3 * chunks * 16, LANES, dtype=bf16),
        (arrived, leave, grad_query, grad_key, grad_value, back, after, came),
        flops=2 * chunks * CHUNK * LANES * 512,
        moved=4 * arrived.size,
        in_specs=[VMEM] * 8,
        out_specs=VMEM,
    )
    if per != 16:
        grads = grads.reshape(16, 3, chunks, 16, LANES).transpose(1, 2, 0, 3, 4)
        grads = grads.reshape(3, chunks, peers, per, LANES).transpose(2, 0, 1, 3, 4)
        grads = grads.reshape(peers, 3 * per_seg, LANES)
    grad_projected = unpack(exchange(grads), rows, heads, segments)
    grad_weight = grad_weight_of(normed, turned)
    return (grad_projected, grad_weight)


def solution(mesh):
    placed = (
        P(("groups", "seq"), None),
        P(("groups", "seq"), None),
        P(("groups", "seq")),
        P(("groups", "seq")),
        P(("groups", "seq")),
        P(("groups", "seq"), None),
        P(),
    )
    return jax.shard_map(
        shards,
        mesh=mesh,
        in_specs=placed,
        out_specs=(P(("groups", "seq"), None), P(("groups", "seq"), None)),
        check_vma=False,
    )
```

```python
import functools

import jax
import jax.numpy as jnp
from jax import lax
from jax.experimental import pallas as pl
from jax.experimental.pallas import tpu as pltpu
from jax.sharding import PartitionSpec as P

norm_eps = 1e-06
LANES = 128
CHUNK = 256
META = 8
bf16 = jnp.bfloat16
f32 = jnp.float32

VMEM = pl.BlockSpec(memory_space=pltpu.VMEM)
SMEM = pl.BlockSpec(memory_space=pltpu.SMEM)
PARAMS = pltpu.CompilerParams(vmem_limit_bytes=24 * 1024 * 1024)
ANY = pl.BlockSpec(memory_space=pl.ANY)


def dot(a, b):
    return lax.dot_general(a, b, (((1,), (0,)), ((), ())), preferred_element_type=f32)


def dot_nt(a, b):
    return lax.dot_general(a, b, (((1,), (1,)), ((), ())), preferred_element_type=f32)


def dot_tn(a, b):
    return lax.dot_general(a, b, (((0,), (0,)), ((), ())), preferred_element_type=f32)


def halves(value):
    high = value.astype(bf16)
    return high, (value - high.astype(f32)).astype(bf16)


def wide(value):
    return jnp.concatenate([value] * (CHUNK // LANES), axis=1)


def iota(shape, dim):
    return lax.broadcasted_iota(jnp.int32, shape, dim)


def call(body, outs, ins, flops=0, moved=0, **more):
    return pl.pallas_call(
        body,
        out_shape=outs,
        compiler_params=PARAMS,
        cost_estimate=pl.CostEstimate(flops=flops, bytes_accessed=moved, transcendentals=0),
        **more,
    )(*ins)


def pack_kernel(heads, segments, rows_ref, decay_ref, starts_ref, out_ref):
    per = rows_ref.shape[0] // segments
    inner = heads * LANES
    decay_rows = decay_ref[...].astype(f32)
    flags = starts_ref[...].astype(f32)
    line = iota((META, LANES), 0)
    for head in range(heads):
        meta = jnp.where(line == 0, decay_rows[head : head + 1, :], jnp.where(line == 1, flags, 0.0))
        for segment in range(segments):
            to = segment * heads + head
            for part in range(3):
                at = part * inner + head * LANES
                out_ref[to, part * per : (part + 1) * per, :] = rows_ref[
                    segment * per : (segment + 1) * per, at : at + LANES
                ]
            out_ref[to, 3 * per :, :] = meta.astype(bf16)


def pack(projected, decay_log, starts, heads, segments):
    rows = projected.shape[0]
    per = rows // segments
    peers = heads * segments
    if per % 16 == 0:
        return call(
            functools.partial(pack_kernel, heads, segments),
            jax.ShapeDtypeStruct((peers, 3 * per + META, LANES), bf16),
            (projected, decay_log.T, starts.reshape(1, rows)),
            moved=4 * projected.size,
            in_specs=[VMEM] * 3,
            out_specs=VMEM,
        )
    body = projected.reshape(segments, per, 3, heads, LANES).transpose(0, 3, 2, 1, 4)
    body = body.reshape(peers, 3 * per, LANES)
    flags = jnp.broadcast_to(starts.astype(bf16)[None, None, :], (heads, 1, rows))
    meta = jnp.concatenate(
        [decay_log.T[:, None, :], flags, jnp.zeros((heads, META - 2, rows), bf16)], axis=1
    )
    meta = jnp.broadcast_to(meta[None], (segments, heads, META, LANES)).reshape(peers, META, LANES)
    return jnp.concatenate([body, meta], axis=1)


def unpack_kernel(heads, segments, in_ref, out_ref):
    per = out_ref.shape[0] // segments
    inner = heads * LANES
    for segment in range(segments):
        for head in range(heads):
            for part in range(3):
                at = part * inner + head * LANES
                out_ref[segment * per : (segment + 1) * per, at : at + LANES] = in_ref[
                    segment * heads + head, part * per : (part + 1) * per, :
                ]


def unpack(arrived, rows, heads, segments):
    per = rows // segments
    if per % 16 == 0:
        return call(
            functools.partial(unpack_kernel, heads, segments),
            jax.ShapeDtypeStruct((rows, 3 * heads * LANES), bf16),
            (arrived,),
            moved=4 * arrived.size,
            in_specs=[VMEM],
            out_specs=VMEM,
        )
    body = arrived.reshape(segments, heads, 3, per, LANES).transpose(0, 3, 2, 1, 4)
    return body.reshape(rows, 3 * heads * LANES)


def turns_of(destination_ref, peers):
    turn = jnp.bitwise_and(destination_ref[...], peers - 1).astype(f32)
    return jnp.broadcast_to(turn, (LANES, LANES)).astype(bf16)


def wrapped(value, peers):
    return jnp.where(value < 0.0, value + peers, jnp.where(value >= peers, value - peers, value))


def places(turns, peers, first, count, rows):
    me = lax.axis_index("seq").astype(f32)
    down = iota((rows, LANES), 0)
    chosen = iota((rows, LANES), 1) == first + down % count
    pick = jnp.where(chosen, 1.0, 0.0).astype(bf16)
    turn = dot_nt(pick, turns) + (down // count).astype(f32) - me
    column = (down % count * peers).astype(f32) + wrapped(turn, peers)
    along = iota((8, rows), 1)
    turn = dot_nt(turns[0:8, :], pick) + (along // count).astype(f32) - me
    line = (along % count * peers).astype(f32) + wrapped(turn, peers)
    return chosen, column, line


def grad_normed_kernel(heads, peers, up_ref, destination_ref, weight_ref, even_ref, odd_ref, turned_ref):
    rows = up_ref.shape[0]
    me = lax.axis_index("seq")
    capacity = rows // peers
    turns = turns_of(destination_ref, peers)
    _, column, _ = places(turns, peers, me * capacity, capacity, rows)
    pick = iota((rows, rows), 1).astype(f32) == column
    turned = dot(jnp.where(pick, 1.0, 0.0).astype(bf16), up_ref[...]).astype(bf16)
    turned_ref[...] = turned
    for step in range(heads):
        head = jnp.bitwise_xor(lax.rem(me, heads), step)
        at = pl.multiple_of(head * LANES, LANES)
        out_ref = odd_ref if step % 2 else even_ref
        out_ref[step // 2] = dot_nt(turned, weight_ref[pl.ds(at, LANES), :])


def grad_normed_of(upstream, destination, out_weight, heads, peers):
    rows, width = upstream.shape
    return call(
        functools.partial(grad_normed_kernel, heads, peers),
        (
            jax.ShapeDtypeStruct((heads // 2, rows, LANES), f32),
            jax.ShapeDtypeStruct((heads // 2, rows, LANES), f32),
            jax.ShapeDtypeStruct((rows, width), bf16),
        ),
        (upstream, destination, out_weight),
        flops=2 * rows * out_weight.size,
        moved=2 * (2 * upstream.size + out_weight.size),
        in_specs=[VMEM] * 3,
        out_specs=[VMEM] * 3,
    )


def grad_weight_kernel(mine_ref, normed_ref, up_ref, out_ref):
    out_ref[...] = dot_tn(normed_ref[0], up_ref[...]).astype(bf16)


def grad_weight_of(normed, upstream, mine):
    heads, rows, _ = normed.shape
    width = upstream.shape[1]
    return call(
        grad_weight_kernel,
        jax.ShapeDtypeStruct((heads * LANES, width), bf16),
        (mine.reshape(1), normed, upstream),
        flops=2 * rows * heads * LANES * width,
        moved=2 * (upstream.size + normed.size + heads * LANES * width),
        grid_spec=pltpu.PrefetchScalarGridSpec(
            num_scalar_prefetch=1,
            grid=(heads,),
            in_specs=[
                pl.BlockSpec((1, rows, LANES), lambda i, mine: (i, 0, 0)),
                pl.BlockSpec((rows, width), lambda i, mine: (0, 0)),
            ],
            out_specs=pl.BlockSpec((LANES, width), lambda i, mine: (jnp.bitwise_xor(mine[0], i), 0)),
        ),
    )


def part_rows(ref, part, chunk):
    per = ref.shape[1] // 3
    if ref.shape[1] % 16:
        per = (ref.shape[1] - META) // 3
    at = part * per + chunk * 16
    return ref[:, at : at + 16, :].reshape(CHUNK, LANES)


class Terms:
    def __init__(self, heads, chunks, meta_ref, destination_ref):
        self.meta_ref = meta_ref
        self.peers = meta_ref.shape[0]
        self.per = CHUNK // self.peers
        self.first_row = lax.axis_index("seq") // heads * self.per * chunks
        self.first_block = lax.axis_index("seq") // heads * heads
        self.turns = turns_of(destination_ref, self.peers)
        lines = self.peers * META
        meta = meta_ref[:, -META:, :].astype(f32).reshape(lines, LANES).astype(bf16)
        row = iota((CHUNK, lines), 0)
        pick = jnp.where(iota((CHUNK, lines), 1) == row // self.per * META, 1.0, 0.0)
        self.decays = dot(pick.astype(bf16), meta)

    def of(self, chunk):
        group = CHUNK // LANES
        chosen, column, line = places(
            self.turns, self.peers, self.first_row + chunk * self.per, self.per, CHUNK
        )
        ones = jnp.ones((LANES, LANES), bf16)
        decay = dot(jnp.where(chosen, self.decays, 0.0).astype(bf16), ones).astype(bf16)
        column = wide(column)
        order = line[0:1, :] <= column
        running = dot(jnp.where(order, 1.0, 0.0).astype(bf16), decay)
        flags = [
            self.meta_ref[self.first_block + chunk * group + i, -META:, :].astype(f32)[1:2, :]
            for i in range(group)
        ]
        flags = jnp.broadcast_to(jnp.concatenate(flags, axis=1), (LANES, CHUNK)).astype(bf16)
        reached = iota((CHUNK, CHUNK), 1).astype(f32) <= column
        count = dot_nt(jnp.where(reached, 1.0, 0.0).astype(bf16), flags)
        last_run = jnp.min(running, axis=0, keepdims=True)
        last_count = jnp.max(count, axis=0, keepdims=True)
        leave = jnp.exp(jnp.minimum(last_run - running, 0.0))
        leave = jnp.where(count == last_count, leave, 0.0)
        total = jnp.where(last_count == 0.0, jnp.exp(last_run), 0.0)
        return order, running, count, leave, total


def state_kernel(heads, chunks, rows_ref, meta_ref, destination_ref, last_ref, keep_ref, gain_ref):
    terms = Terms(heads, chunks, meta_ref, destination_ref)
    state = jnp.zeros((LANES, LANES), f32)
    before = jnp.ones((1, LANES), f32)
    line = iota((8, LANES), 0)
    for chunk in range(chunks):
        _, _, _, leave, total = terms.of(chunk)
        key, value = (part_rows(rows_ref, part, chunk) for part in (1, 2))
        high, low = halves(key.astype(f32) * leave)
        keep_ref[chunk, 0:LANES, :] = state
        keep_ref[chunk, LANES:, :] = jnp.where(line == 0, before, total)
        state = total * state + dot_tn(high, value) + dot_tn(low, value)
        before = total * before
    last_ref[...] = state
    gain_ref[...] = jnp.broadcast_to(before, (8, LANES))


def inner_kernel(
    heads, chunks, rows_ref, meta_ref, destination_ref, mix_ref, weights_ref, inner_ref, ends_ref
):
    terms = Terms(heads, chunks, meta_ref, destination_ref)
    lane = iota((CHUNK, LANES), 1)
    for chunk in range(chunks):
        order, running, count, leave, _ = terms.of(chunk)
        turned = jnp.where(lane == 0, running, count).T
        same = order & (wide(count) == turned[1:2, :])
        gap = jnp.minimum(wide(running) - turned[0:1, :], 0.0)
        mix = jnp.where(same, jnp.exp(gap), 0.0)
        enter = jnp.where(count == 0.0, jnp.exp(running), 0.0)
        query, key, value = (part_rows(rows_ref, part, chunk) for part in range(3))
        weights = (dot_nt(query, key) * mix).astype(bf16)
        mix_ref[chunk] = mix
        weights_ref[chunk] = weights
        inner_ref[chunk] = dot(weights, value)
        ends_ref[chunk] = jnp.where(lane == 0, enter, leave)


def entering(keep_ref, chunk, came):
    keep = keep_ref[chunk]
    return halves(keep[0:LANES, :] + keep[LANES : LANES + 1, :] * came), keep[LANES + 1 : LANES + 2, :]


def output_kernel(
    heads, chunks, runs, rows_ref, inner_ref, ends_ref, keep_ref, came_ref, *refs
):
    given, (grad_ref, block_ref, back_ref, last_ref, normal_ref, sems) = refs[:-6], refs[-6:]
    mine = lax.rem(lax.axis_index("seq"), heads)
    sources = [given[0].at[0], given[1].at[0]]
    for pair in given[2:]:
        sources += [pair.at[0], pair.at[1]]
    copies = [
        pltpu.make_async_copy(
            source, normal_ref.at[jnp.bitwise_xor(mine, step)], sems.at[step]
        )
        for step, source in enumerate(sources)
    ]
    for copy in copies:
        copy.start()
    group = CHUNK // LANES
    back = jnp.zeros((LANES, LANES), f32)
    after = jnp.ones((1, LANES), f32)
    line = iota((8, LANES), 0)
    came = came_ref[...]
    normed_rows = []
    for chunk in range(chunks):
        query = part_rows(rows_ref, 0, chunk)
        enter = ends_ref[chunk][:, 0:1]
        (high, low), _ = entering(keep_ref, chunk, came)
        output = inner_ref[chunk] + enter * (dot(query, high) + dot(query, low))
        scale = lax.rsqrt(jnp.mean(output * output, axis=1, keepdims=True) + norm_eps)
        normed = output * scale
        split = normed.reshape(runs, group, CHUNK // (runs * group), LANES)
        for i in range(group):
            step = jnp.bitwise_xor(mine, chunk * group + i)
            at = jnp.bitwise_and(step, 1) * (heads // 2) + lax.div(step, 2)
            block_ref[at] = split[:, i].reshape(LANES, LANES).astype(bf16)
        normed_rows.append((normed, scale))
    for copy in copies:
        copy.wait()
    for chunk in reversed(range(chunks)):
        normed, scale = normed_rows[chunk]
        query = part_rows(rows_ref, 0, chunk)
        enter = ends_ref[chunk][:, 0:1]
        normal = jnp.concatenate(
            [
                normal_ref[chunk * group + i].reshape(runs, 1, CHUNK // (runs * group), LANES)
                for i in range(group)
            ],
            axis=1,
        ).reshape(CHUNK, LANES)
        grad = (
            (normal - normed * jnp.mean(normal * normed, axis=1, keepdims=True)) * scale
        ).astype(bf16)
        grad_ref[chunk] = grad
        gain = keep_ref[chunk, LANES + 1 : LANES + 2, :]
        back_ref[chunk, 0:LANES, :] = back
        back_ref[chunk, LANES:, :] = jnp.where(line == 0, after, gain)
        high, low = halves(query.astype(f32) * enter)
        back = gain * back + dot_tn(high, grad) + dot_tn(low, grad)
        after = gain * after
    last_ref[...] = back


def local_kernel(
    chunks, rows_ref, mix_ref, weights_ref, ends_ref, keep_ref, came_ref, grad_ref, query_ref, part_ref
):
    came = came_ref[...]
    for chunk in range(chunks):
        query, key, value = (part_rows(rows_ref, part, chunk) for part in range(3))
        grad = grad_ref[chunk]
        (high, low), _ = entering(keep_ref, chunk, came)
        grad_mix = (dot_nt(grad, value) * mix_ref[chunk]).astype(bf16)
        grad_query = dot_nt(grad, high) + dot_nt(grad, low)
        grad_query = dot(grad_mix, key) + ends_ref[chunk][:, 0:1] * grad_query
        query_ref[:, chunk * 16 : (chunk + 1) * 16, :] = (
            grad_query.astype(bf16).reshape(16, 16, LANES)
        )
        part_ref[0, chunk] = dot_tn(grad_mix, query)
        part_ref[1, chunk] = dot_tn(weights_ref[chunk], grad)


def final_kernel(chunks, rows_ref, ends_ref, query_ref, part_ref, back_ref, came_ref, out_ref):
    per = chunks * 16
    came = came_ref[...]
    out_ref[:, 0:per, :] = query_ref[...]
    for chunk in range(chunks):
        key, value = (part_rows(rows_ref, part, chunk) for part in (1, 2))
        leave = ends_ref[chunk][:, 1:2]
        (high, low), _ = entering(back_ref, chunk, came)
        grad_key = part_ref[0, chunk] + leave * (dot_nt(value, high) + dot_nt(value, low))
        grad_value = part_ref[1, chunk] + leave * (dot(key, high) + dot(key, low))
        for part, grad in ((1, grad_key), (2, grad_value)):
            at = part * per + chunk * 16
            out_ref[:, at : at + 16, :] = grad.astype(bf16).reshape(16, 16, LANES)


def carried(last, gain, segments, heads, step):
    def shift(value, by):
        pairs = [
            (s * heads + h, (s + by * step) * heads + h)
            for s in range(segments)
            for h in range(heads)
            if 0 <= s + by * step < segments
        ]
        return lax.ppermute(value, "seq", pairs)

    state = shift(last, 1)
    if segments > 2:
        gain = shift(gain, 1)
        by = 1
        while by < segments - 1:
            state, gain = state + gain[0:1, :] * shift(state, by), gain * shift(gain, by)
            by *= 2
    return state


def shards(projected, decay_log, destination, source, starts, upstream, out_weight):
    rows = projected.shape[0]
    heads = decay_log.shape[1]
    peers = lax.axis_size("seq")
    segments = peers // heads
    per_seg = rows // segments
    chunks = heads * rows // CHUNK
    per = CHUNK // peers
    me = lax.axis_index("seq")
    segment = me // heads
    groups = [[s * heads + h for h in range(heads)] for s in range(segments)]

    def exchange(value):
        return lax.all_to_all(value, "seq", split_axis=0, concat_axis=0, tiled=True)

    def among_heads(value):
        return lax.all_to_all(
            value, "seq", split_axis=0, concat_axis=0, tiled=True, axis_index_groups=groups
        )

    place = destination.reshape(1, rows)
    arrived = exchange(pack(projected, decay_log, starts, heads, segments))
    even, odd, turned = grad_normed_of(upstream, place, out_weight, heads, peers)
    mine = me % heads
    steps = [jnp.bitwise_xor(mine, step) for step in range(heads)]

    def swap(value, step):
        return lax.ppermute(value, "seq", [(i, i ^ step) for i in range(peers)])

    def deal(even, odd):
        other = swap(odd, 1)
        pairs = [
            swap(jnp.stack([even[step], other[step]]), 2 * step) for step in range(1, heads // 2)
        ]
        return [even[0:1], other[0:1], *pairs]

    if per == 16:
        runs = peers
        meta = arrived
        normal = deal(even, odd)
    else:
        runs = 1
        meta = arrived[:, 3 * per_seg :, :]
        arrived = arrived[:, : 3 * per_seg, :].reshape(peers, 3, chunks, per, LANES)
        arrived = arrived.transpose(1, 2, 0, 3, 4).reshape(3, chunks, 16, 16, LANES)
        arrived = arrived.transpose(2, 0, 1, 3, 4).reshape(16, 3 * chunks * 16, LANES)
        normal = jnp.stack([even, odd], axis=1).reshape(heads, rows, LANES)
        normal = among_heads(jnp.stack([normal[step] for step in steps]))
        normal = normal.reshape(chunks, CHUNK // rows, peers, rows // peers, LANES)
        normal = normal.swapaxes(1, 2).reshape(heads, rows, LANES)
        normal = jnp.stack([normal[step] for step in steps])
        normal = [normal[0:1], normal[1:2], *(normal[i : i + 2] for i in range(2, heads, 2))]

    def shape(*dims, dtype=f32):
        return jax.ShapeDtypeStruct(dims, dtype)

    tall = (chunks, CHUNK, LANES)
    square = (chunks, CHUNK, CHUNK)
    states = (chunks, LANES + 8, LANES)
    low = (16, chunks * 16, LANES)
    unit = 2 * chunks * CHUNK * LANES
    last, keep, gain = call(
        functools.partial(state_kernel, heads, chunks),
        (shape(LANES, LANES), shape(*states), shape(8, LANES)),
        (arrived, meta, place),
        flops=unit * 512,
        moved=2 * arrived.size,
        in_specs=[VMEM] * 3,
        out_specs=[VMEM] * 3,
    )
    came = carried(last, gain, segments, heads, 1)
    mix, weights, inner, ends = call(
        functools.partial(inner_kernel, heads, chunks),
        (shape(*square), shape(*square, dtype=bf16), shape(*tall), shape(*tall)),
        (arrived, meta, place),
        flops=unit * 1024,
        moved=2 * arrived.size + 8 * chunks * CHUNK * CHUNK,
        in_specs=[VMEM] * 3,
        out_specs=[VMEM] * 4,
    )
    grad, normed, back, last = call(
        functools.partial(output_kernel, heads, chunks, runs),
        (
            shape(*tall, dtype=bf16), shape(heads, rows, LANES, dtype=bf16), shape(*states),
            shape(LANES, LANES),
        ),
        (arrived, inner, ends, keep, came, *normal),
        flops=unit * 1024,
        moved=2 * arrived.size + 8 * chunks * CHUNK * LANES,
        in_specs=[VMEM] * 5 + [ANY] * len(normal),
        out_specs=[VMEM] * 4,
        scratch_shapes=[
            pltpu.VMEM((heads, rows, LANES), f32),
            pltpu.SemaphoreType.DMA((heads,)),
        ],
    )
    came_back = carried(last, gain, segments, heads, -1)
    grad_query, part = call(
        functools.partial(local_kernel, chunks),
        (shape(*low, dtype=bf16), shape(2, *tall)),
        (arrived, mix, weights, ends, keep, came, grad),
        flops=unit * 1024,
        moved=2 * arrived.size + 8 * chunks * CHUNK * CHUNK,
        in_specs=[VMEM] * 7,
        out_specs=[VMEM] * 2,
    )
    grads = call(
        functools.partial(final_kernel, chunks),
        shape(16, 3 * chunks * 16, LANES, dtype=bf16),
        (arrived, ends, grad_query, part, back, came_back),
        flops=unit * 512,
        moved=4 * arrived.size,
        in_specs=[VMEM] * 6,
        out_specs=VMEM,
    )
    normed, grads = lax.optimization_barrier((normed, grads))
    if per == 16:
        normed = jnp.concatenate(deal(normed[: heads // 2], normed[heads // 2 :]))
    else:
        normed = normed.reshape(2, heads // 2, rows, LANES).swapaxes(0, 1)
        normed = normed.reshape(heads, rows, LANES)
        normed = jnp.stack([normed[step] for step in steps])
        normed = normed.reshape(chunks, peers, CHUNK // rows, rows // peers, LANES)
        normed = among_heads(normed.swapaxes(1, 2).reshape(heads, rows, LANES))
        normed = jnp.stack([normed[step] for step in steps])
        grads = grads.reshape(16, 3, chunks, 16, LANES).transpose(1, 2, 0, 3, 4)
        grads = grads.reshape(3, chunks, peers, per, LANES).transpose(2, 0, 1, 3, 4)
        grads = grads.reshape(peers, 3 * per_seg, LANES)
    grad_projected = unpack(exchange(grads), rows, heads, segments)
    grad_weight = grad_weight_of(normed, turned, mine)
    return (grad_projected, grad_weight)


def solution(mesh):
    placed = (
        P(("groups", "seq"), None),
        P(("groups", "seq"), None),
        P(("groups", "seq")),
        P(("groups", "seq")),
        P(("groups", "seq")),
        P(("groups", "seq"), None),
        P(),
    )
    return jax.shard_map(
        shards,
        mesh=mesh,
        in_specs=placed,
        out_specs=(P(("groups", "seq"), None), P(("groups", "seq"), None)),
        check_vma=False,
    )
```

```python
import functools

import jax
import jax.numpy as jnp
from jax import lax
from jax.experimental import pallas as pl
from jax.experimental.pallas import tpu as pltpu
from jax.sharding import PartitionSpec as P

norm_eps = 1e-06
LANES = 128
CHUNK = 256
META = 8
bf16 = jnp.bfloat16
f32 = jnp.float32

VMEM = pl.BlockSpec(memory_space=pltpu.VMEM)
SMEM = pl.BlockSpec(memory_space=pltpu.SMEM)
PARAMS = pltpu.CompilerParams(vmem_limit_bytes=24 * 1024 * 1024)
ANY = pl.BlockSpec(memory_space=pl.ANY)


def dot(a, b):
    return lax.dot_general(a, b, (((1,), (0,)), ((), ())), preferred_element_type=f32)


def dot_nt(a, b):
    return lax.dot_general(a, b, (((1,), (1,)), ((), ())), preferred_element_type=f32)


def dot_tn(a, b):
    return lax.dot_general(a, b, (((0,), (0,)), ((), ())), preferred_element_type=f32)


def halves(value):
    high = value.astype(bf16)
    return high, (value - high.astype(f32)).astype(bf16)


def wide(value):
    return jnp.concatenate([value] * (CHUNK // LANES), axis=1)


def iota(shape, dim):
    return lax.broadcasted_iota(jnp.int32, shape, dim)


def call(body, outs, ins, flops=0, moved=0, **more):
    return pl.pallas_call(
        body,
        out_shape=outs,
        compiler_params=PARAMS,
        cost_estimate=pl.CostEstimate(flops=flops, bytes_accessed=moved, transcendentals=0),
        **more,
    )(*ins)


def pack_kernel(heads, segments, rows_ref, decay_ref, starts_ref, out_ref):
    per = rows_ref.shape[0] // segments
    inner = heads * LANES
    decay_rows = decay_ref[...].astype(f32)
    flags = starts_ref[...].astype(f32)
    line = iota((META, LANES), 0)
    for head in range(heads):
        meta = jnp.where(line == 0, decay_rows[head : head + 1, :], jnp.where(line == 1, flags, 0.0))
        for segment in range(segments):
            to = segment * heads + head
            for part in range(3):
                at = part * inner + head * LANES
                out_ref[to, part * per : (part + 1) * per, :] = rows_ref[
                    segment * per : (segment + 1) * per, at : at + LANES
                ]
            out_ref[to, 3 * per :, :] = meta.astype(bf16)


def pack(projected, decay_log, starts, heads, segments):
    rows = projected.shape[0]
    per = rows // segments
    peers = heads * segments
    if per % 16 == 0:
        return call(
            functools.partial(pack_kernel, heads, segments),
            jax.ShapeDtypeStruct((peers, 3 * per + META, LANES), bf16),
            (projected, decay_log.T, starts.reshape(1, rows)),
            moved=4 * projected.size,
            in_specs=[VMEM] * 3,
            out_specs=VMEM,
        )
    body = projected.reshape(segments, per, 3, heads, LANES).transpose(0, 3, 2, 1, 4)
    body = body.reshape(peers, 3 * per, LANES)
    flags = jnp.broadcast_to(starts.astype(bf16)[None, None, :], (heads, 1, rows))
    meta = jnp.concatenate(
        [decay_log.T[:, None, :], flags, jnp.zeros((heads, META - 2, rows), bf16)], axis=1
    )
    meta = jnp.broadcast_to(meta[None], (segments, heads, META, LANES)).reshape(peers, META, LANES)
    return jnp.concatenate([body, meta], axis=1)


def unpack_kernel(heads, segments, in_ref, out_ref):
    per = out_ref.shape[0] // segments
    inner = heads * LANES
    for segment in range(segments):
        for head in range(heads):
            for part in range(3):
                at = part * inner + head * LANES
                out_ref[segment * per : (segment + 1) * per, at : at + LANES] = in_ref[
                    segment * heads + head, part * per : (part + 1) * per, :
                ]


def unpack(arrived, rows, heads, segments):
    per = rows // segments
    if per % 16 == 0:
        return call(
            functools.partial(unpack_kernel, heads, segments),
            jax.ShapeDtypeStruct((rows, 3 * heads * LANES), bf16),
            (arrived,),
            moved=4 * arrived.size,
            in_specs=[VMEM],
            out_specs=VMEM,
        )
    body = arrived.reshape(segments, heads, 3, per, LANES).transpose(0, 3, 2, 1, 4)
    return body.reshape(rows, 3 * heads * LANES)


def turns_of(destination_ref, peers):
    turn = jnp.bitwise_and(destination_ref[...], peers - 1).astype(f32)
    return jnp.broadcast_to(turn, (LANES, LANES)).astype(bf16)


def wrapped(value, peers):
    return jnp.where(value < 0.0, value + peers, jnp.where(value >= peers, value - peers, value))


def places(turns, peers, first, count, rows):
    me = lax.axis_index("seq").astype(f32)
    down = iota((rows, LANES), 0)
    chosen = iota((rows, LANES), 1) == first + down % count
    pick = jnp.where(chosen, 1.0, 0.0).astype(bf16)
    turn = dot_nt(pick, turns) + (down // count).astype(f32) - me
    column = (down % count * peers).astype(f32) + wrapped(turn, peers)
    along = iota((8, rows), 1)
    turn = dot_nt(turns[0:8, :], pick) + (along // count).astype(f32) - me
    line = (along % count * peers).astype(f32) + wrapped(turn, peers)
    return chosen, column, line


def grad_normed_kernel(heads, peers, up_ref, destination_ref, weight_ref, even_ref, odd_ref, turned_ref):
    rows = up_ref.shape[0]
    me = lax.axis_index("seq")
    capacity = rows // peers
    turns = turns_of(destination_ref, peers)
    _, column, _ = places(turns, peers, me * capacity, capacity, rows)
    pick = iota((rows, rows), 1).astype(f32) == column
    turned = dot(jnp.where(pick, 1.0, 0.0).astype(bf16), up_ref[...]).astype(bf16)
    turned_ref[...] = turned
    for step in range(heads):
        head = jnp.bitwise_xor(lax.rem(me, heads), step)
        at = pl.multiple_of(head * LANES, LANES)
        out_ref = odd_ref if step % 2 else even_ref
        out_ref[step // 2] = dot_nt(turned, weight_ref[pl.ds(at, LANES), :])


def grad_normed_of(upstream, destination, out_weight, heads, peers):
    rows, width = upstream.shape
    return call(
        functools.partial(grad_normed_kernel, heads, peers),
        (
            jax.ShapeDtypeStruct((heads // 2, rows, LANES), f32),
            jax.ShapeDtypeStruct((heads // 2, rows, LANES), f32),
            jax.ShapeDtypeStruct((rows, width), bf16),
        ),
        (upstream, destination, out_weight),
        flops=2 * rows * out_weight.size,
        moved=2 * (2 * upstream.size + out_weight.size),
        in_specs=[VMEM] * 3,
        out_specs=[VMEM] * 3,
    )


def grad_weight_of(normed, upstream, heads, mine):
    rows, width = upstream.shape
    total = jax.ShapeDtypeStruct((heads * LANES, width), bf16)
    calls = [normed[:2]] + [[pair] for pair in normed[2:]]
    out = None
    for at, pieces in enumerate(calls):
        count = sum(piece.shape[0] for piece in pieces)

        def body(mine_ref, *refs):
            *piece_refs, up_ref, out_ref = refs[: len(pieces) + 1] + refs[-1:]
            step = pl.program_id(0)
            first = 0
            for piece_ref in piece_refs:
                for i in range(piece_ref.shape[0]):

                    @pl.when(step == first)
                    def _(piece_ref=piece_ref, i=i):
                        out_ref[...] = dot_tn(piece_ref[i], up_ref[...]).astype(bf16)

                    first += 1

        given = [] if out is None else [out]
        out = pl.pallas_call(
            body,
            out_shape=total,
            grid_spec=pltpu.PrefetchScalarGridSpec(
                num_scalar_prefetch=1,
                grid=(count,),
                in_specs=[
                    pl.BlockSpec(piece.shape, lambda i, mine: (0, 0, 0)) for piece in pieces
                ]
                + [pl.BlockSpec((rows, width), lambda i, mine: (0, 0))]
                + [ANY for _ in given],
                out_specs=pl.BlockSpec(
                    (LANES, width),
                    lambda i, mine, at=at: (jnp.bitwise_xor(mine[0], 2 * at + i), 0),
                ),
            ),
            input_output_aliases={len(pieces) + 2: 0} if given else {},
            compiler_params=PARAMS,
            cost_estimate=pl.CostEstimate(
                flops=2 * rows * count * LANES * width,
                bytes_accessed=2 * count * LANES * width,
                transcendentals=0,
            ),
        )(mine.reshape(1), *pieces, upstream, *given)
    return out


def part_rows(ref, part, chunk):
    per = ref.shape[1] // 3
    if ref.shape[1] % 16:
        per = (ref.shape[1] - META) // 3
    at = part * per + chunk * 16
    return ref[:, at : at + 16, :].reshape(CHUNK, LANES)


class Terms:
    def __init__(self, heads, chunks, meta_ref, destination_ref):
        self.meta_ref = meta_ref
        self.peers = meta_ref.shape[0]
        self.per = CHUNK // self.peers
        self.first_row = lax.axis_index("seq") // heads * self.per * chunks
        self.first_block = lax.axis_index("seq") // heads * heads
        self.turns = turns_of(destination_ref, self.peers)
        lines = self.peers * META
        meta = meta_ref[:, -META:, :].astype(f32).reshape(lines, LANES).astype(bf16)
        row = iota((CHUNK, lines), 0)
        pick = jnp.where(iota((CHUNK, lines), 1) == row // self.per * META, 1.0, 0.0)
        self.decays = dot(pick.astype(bf16), meta)

    def of(self, chunk):
        group = CHUNK // LANES
        chosen, column, line = places(
            self.turns, self.peers, self.first_row + chunk * self.per, self.per, CHUNK
        )
        ones = jnp.ones((LANES, LANES), bf16)
        decay = dot(jnp.where(chosen, self.decays, 0.0).astype(bf16), ones).astype(bf16)
        column = wide(column)
        order = line[0:1, :] <= column
        running = dot(jnp.where(order, 1.0, 0.0).astype(bf16), decay)
        flags = [
            self.meta_ref[self.first_block + chunk * group + i, -META:, :].astype(f32)[1:2, :]
            for i in range(group)
        ]
        flags = jnp.broadcast_to(jnp.concatenate(flags, axis=1), (LANES, CHUNK)).astype(bf16)
        reached = iota((CHUNK, CHUNK), 1).astype(f32) <= column
        count = dot_nt(jnp.where(reached, 1.0, 0.0).astype(bf16), flags)
        last_run = jnp.min(running, axis=0, keepdims=True)
        last_count = jnp.max(count, axis=0, keepdims=True)
        leave = jnp.exp(jnp.minimum(last_run - running, 0.0))
        leave = jnp.where(count == last_count, leave, 0.0)
        total = jnp.where(last_count == 0.0, jnp.exp(last_run), 0.0)
        return order, running, count, leave, total


def state_kernel(heads, chunks, rows_ref, meta_ref, destination_ref, last_ref, keep_ref, gain_ref):
    terms = Terms(heads, chunks, meta_ref, destination_ref)
    state = jnp.zeros((LANES, LANES), f32)
    before = jnp.ones((1, LANES), f32)
    line = iota((8, LANES), 0)
    for chunk in range(chunks):
        _, _, _, leave, total = terms.of(chunk)
        key, value = (part_rows(rows_ref, part, chunk) for part in (1, 2))
        high, low = halves(key.astype(f32) * leave)
        keep_ref[chunk, 0:LANES, :] = state
        keep_ref[chunk, LANES:, :] = jnp.where(line == 0, before, total)
        state = total * state + dot_tn(high, value) + dot_tn(low, value)
        before = total * before
    last_ref[...] = state.astype(bf16)
    gain_ref[...] = jnp.broadcast_to(before, (8, LANES))


def inner_kernel(
    heads, chunks, rows_ref, meta_ref, destination_ref, mix_ref, weights_ref, inner_ref, ends_ref
):
    terms = Terms(heads, chunks, meta_ref, destination_ref)
    lane = iota((CHUNK, LANES), 1)
    for chunk in range(chunks):
        order, running, count, leave, _ = terms.of(chunk)
        turned = jnp.where(lane == 0, running, count).T
        same = order & (wide(count) == turned[1:2, :])
        gap = jnp.minimum(wide(running) - turned[0:1, :], 0.0)
        mix = jnp.where(same, jnp.exp(gap), 0.0)
        enter = jnp.where(count == 0.0, jnp.exp(running), 0.0)
        query, key, value = (part_rows(rows_ref, part, chunk) for part in range(3))
        weights = (dot_nt(query, key) * mix).astype(bf16)
        mix_ref[chunk] = mix
        weights_ref[chunk] = weights
        inner_ref[chunk] = dot(weights, value)
        ends_ref[chunk] = jnp.where(lane == 0, enter, leave)


def arriving(came_ref, heads, step):
    segment = lax.div(lax.axis_index("seq"), heads)
    last = lax.div(lax.axis_size("seq"), heads) - 1
    end = 0 if step == 1 else last
    return jnp.where(segment == end, 0.0, came_ref[...].astype(f32))


def entering(keep_ref, chunk, came):
    keep = keep_ref[chunk]
    return halves(keep[0:LANES, :] + keep[LANES : LANES + 1, :] * came), keep[LANES + 1 : LANES + 2, :]


def output_kernel(
    heads, chunks, runs, rows_ref, inner_ref, ends_ref, keep_ref, came_ref, *refs
):
    given, (grad_ref, block_ref, back_ref, last_ref, normal_ref, sems) = refs[:-6], refs[-6:]
    mine = lax.rem(lax.axis_index("seq"), heads)
    sources = [given[0].at[0], given[1].at[0]]
    for pair in given[2:]:
        sources += [pair.at[0], pair.at[1]]
    copies = [
        pltpu.make_async_copy(
            source, normal_ref.at[jnp.bitwise_xor(mine, step)], sems.at[step]
        )
        for step, source in enumerate(sources)
    ]
    for copy in copies:
        copy.start()
    group = CHUNK // LANES
    back = jnp.zeros((LANES, LANES), f32)
    after = jnp.ones((1, LANES), f32)
    line = iota((8, LANES), 0)
    came = arriving(came_ref, heads, 1)
    normed_rows = []
    for chunk in range(chunks):
        query = part_rows(rows_ref, 0, chunk)
        enter = ends_ref[chunk][:, 0:1]
        (high, low), _ = entering(keep_ref, chunk, came)
        output = inner_ref[chunk] + enter * (dot(query, high) + dot(query, low))
        scale = lax.rsqrt(jnp.mean(output * output, axis=1, keepdims=True) + norm_eps)
        normed = output * scale
        split = normed.reshape(runs, group, CHUNK // (runs * group), LANES)
        for i in range(group):
            step = jnp.bitwise_xor(mine, chunk * group + i)
            at = jnp.bitwise_and(step, 1) * (heads // 2) + lax.div(step, 2)
            block_ref[at] = split[:, i].reshape(LANES, LANES).astype(bf16)
        normed_rows.append((normed, scale))
    for copy in copies:
        copy.wait()
    for chunk in reversed(range(chunks)):
        normed, scale = normed_rows[chunk]
        query = part_rows(rows_ref, 0, chunk)
        enter = ends_ref[chunk][:, 0:1]
        normal = jnp.concatenate(
            [
                normal_ref[chunk * group + i].reshape(runs, 1, CHUNK // (runs * group), LANES)
                for i in range(group)
            ],
            axis=1,
        ).reshape(CHUNK, LANES)
        grad = (
            (normal - normed * jnp.mean(normal * normed, axis=1, keepdims=True)) * scale
        ).astype(bf16)
        grad_ref[chunk] = grad
        gain = keep_ref[chunk, LANES + 1 : LANES + 2, :]
        back_ref[chunk, 0:LANES, :] = back
        back_ref[chunk, LANES:, :] = jnp.where(line == 0, after, gain)
        high, low = halves(query.astype(f32) * enter)
        back = gain * back + dot_tn(high, grad) + dot_tn(low, grad)
        after = gain * after
    last_ref[...] = back.astype(bf16)


def local_kernel(
    heads, chunks, rows_ref, mix_ref, weights_ref, ends_ref, keep_ref, came_ref, grad_ref, query_ref, part_ref
):
    came = arriving(came_ref, heads, 1)
    for chunk in range(chunks):
        query, key, value = (part_rows(rows_ref, part, chunk) for part in range(3))
        grad = grad_ref[chunk]
        (high, low), _ = entering(keep_ref, chunk, came)
        grad_mix = (dot_nt(grad, value) * mix_ref[chunk]).astype(bf16)
        grad_query = dot_nt(grad, high) + dot_nt(grad, low)
        grad_query = dot(grad_mix, key) + ends_ref[chunk][:, 0:1] * grad_query
        query_ref[:, chunk * 16 : (chunk + 1) * 16, :] = (
            grad_query.astype(bf16).reshape(16, 16, LANES)
        )
        part_ref[0, chunk] = dot_tn(grad_mix, query)
        part_ref[1, chunk] = dot_tn(weights_ref[chunk], grad)


def final_kernel(heads, chunks, rows_ref, ends_ref, query_ref, part_ref, back_ref, came_ref, out_ref):
    per = chunks * 16
    came = arriving(came_ref, heads, -1)
    out_ref[:, 0:per, :] = query_ref[...]
    for chunk in range(chunks):
        key, value = (part_rows(rows_ref, part, chunk) for part in (1, 2))
        leave = ends_ref[chunk][:, 1:2]
        (high, low), _ = entering(back_ref, chunk, came)
        grad_key = part_ref[0, chunk] + leave * (dot_nt(value, high) + dot_nt(value, low))
        grad_value = part_ref[1, chunk] + leave * (dot(key, high) + dot(key, low))
        for part, grad in ((1, grad_key), (2, grad_value)):
            at = part * per + chunk * 16
            out_ref[:, at : at + 16, :] = grad.astype(bf16).reshape(16, 16, LANES)


def carried(last, gain, segments, heads, step):
    if segments == 2:
        pairs = [(i, (i + heads) % (2 * heads)) for i in range(2 * heads)]
        return lax.ppermute(last, "seq", pairs)

    def shift(value, by):
        pairs = [
            (s * heads + h, (s + by * step) * heads + h)
            for s in range(segments)
            for h in range(heads)
            if 0 <= s + by * step < segments
        ]
        return lax.ppermute(value, "seq", pairs)

    state = shift(last, 1)
    if segments > 2:
        gain = shift(gain, 1)
        by = 1
        while by < segments - 1:
            state, gain = state + gain[0:1, :] * shift(state, by), gain * shift(gain, by)
            by *= 2
    return state


def shards(projected, decay_log, destination, source, starts, upstream, out_weight):
    rows = projected.shape[0]
    heads = decay_log.shape[1]
    peers = lax.axis_size("seq")
    segments = peers // heads
    per_seg = rows // segments
    chunks = heads * rows // CHUNK
    per = CHUNK // peers
    me = lax.axis_index("seq")
    segment = me // heads
    groups = [[s * heads + h for h in range(heads)] for s in range(segments)]

    def exchange(value):
        return lax.all_to_all(value, "seq", split_axis=0, concat_axis=0, tiled=True)

    def among_heads(value):
        return lax.all_to_all(
            value, "seq", split_axis=0, concat_axis=0, tiled=True, axis_index_groups=groups
        )

    place = destination.reshape(1, rows)
    arrived = exchange(pack(projected, decay_log, starts, heads, segments))
    even, odd, turned = grad_normed_of(upstream, place, out_weight, heads, peers)
    mine = me % heads
    steps = [jnp.bitwise_xor(mine, step) for step in range(heads)]

    def swap(value, step):
        return lax.ppermute(value, "seq", [(i, i ^ step) for i in range(peers)])

    def deal(even, odd):
        other = swap(odd, 1)
        pairs = [
            swap(jnp.stack([even[step], other[step]]), 2 * step) for step in range(1, heads // 2)
        ]
        return [even[0:1], other[0:1], *pairs]

    if per == 16:
        runs = peers
        meta = arrived
        normal = deal(even, odd)
    else:
        runs = 1
        meta = arrived[:, 3 * per_seg :, :]
        arrived = arrived[:, : 3 * per_seg, :].reshape(peers, 3, chunks, per, LANES)
        arrived = arrived.transpose(1, 2, 0, 3, 4).reshape(3, chunks, 16, 16, LANES)
        arrived = arrived.transpose(2, 0, 1, 3, 4).reshape(16, 3 * chunks * 16, LANES)
        normal = jnp.stack([even, odd], axis=1).reshape(heads, rows, LANES)
        normal = among_heads(jnp.stack([normal[step] for step in steps]))
        normal = normal.reshape(chunks, CHUNK // rows, peers, rows // peers, LANES)
        normal = normal.swapaxes(1, 2).reshape(heads, rows, LANES)
        normal = jnp.stack([normal[step] for step in steps])
        normal = [normal[0:1], normal[1:2], *(normal[i : i + 2] for i in range(2, heads, 2))]

    def shape(*dims, dtype=f32):
        return jax.ShapeDtypeStruct(dims, dtype)

    tall = (chunks, CHUNK, LANES)
    square = (chunks, CHUNK, CHUNK)
    states = (chunks, LANES + 8, LANES)
    low = (16, chunks * 16, LANES)
    unit = 2 * chunks * CHUNK * LANES
    last, keep, gain = call(
        functools.partial(state_kernel, heads, chunks),
        (shape(LANES, LANES, dtype=bf16), shape(*states), shape(8, LANES)),
        (arrived, meta, place),
        flops=unit * 512,
        moved=2 * arrived.size,
        in_specs=[VMEM] * 3,
        out_specs=[VMEM] * 3,
    )
    came = carried(last, gain, segments, heads, 1)
    mix, weights, inner, ends = call(
        functools.partial(inner_kernel, heads, chunks),
        (shape(*square), shape(*square, dtype=bf16), shape(*tall), shape(*tall)),
        (arrived, meta, place),
        flops=unit * 1024,
        moved=2 * arrived.size + 8 * chunks * CHUNK * CHUNK,
        in_specs=[VMEM] * 3,
        out_specs=[VMEM] * 4,
    )
    grad, normed, back, last = call(
        functools.partial(output_kernel, heads, chunks, runs),
        (
            shape(*tall, dtype=bf16), shape(heads, rows, LANES, dtype=bf16), shape(*states),
            shape(LANES, LANES, dtype=bf16),
        ),
        (arrived, inner, ends, keep, came, *normal),
        flops=unit * 1024,
        moved=2 * arrived.size + 8 * chunks * CHUNK * LANES,
        in_specs=[VMEM] * 5 + [ANY] * len(normal),
        out_specs=[VMEM] * 4,
        scratch_shapes=[
            pltpu.VMEM((heads, rows, LANES), f32),
            pltpu.SemaphoreType.DMA((heads,)),
        ],
    )
    came_back = carried(last, gain, segments, heads, -1)
    grad_query, part = call(
        functools.partial(local_kernel, heads, chunks),
        (shape(*low, dtype=bf16), shape(2, *tall)),
        (arrived, mix, weights, ends, keep, came, grad),
        flops=unit * 1024,
        moved=2 * arrived.size + 8 * chunks * CHUNK * CHUNK,
        in_specs=[VMEM] * 7,
        out_specs=[VMEM] * 2,
    )
    grads = call(
        functools.partial(final_kernel, heads, chunks),
        shape(16, 3 * chunks * 16, LANES, dtype=bf16),
        (arrived, ends, grad_query, part, back, came_back),
        flops=unit * 512,
        moved=4 * arrived.size,
        in_specs=[VMEM] * 6,
        out_specs=VMEM,
    )
    normed, grads = lax.optimization_barrier((normed, grads))
    if per == 16:
        normed = deal(normed[: heads // 2], normed[heads // 2 :])
    else:
        normed = normed.reshape(2, heads // 2, rows, LANES).swapaxes(0, 1)
        normed = normed.reshape(heads, rows, LANES)
        normed = jnp.stack([normed[step] for step in steps])
        normed = normed.reshape(chunks, peers, CHUNK // rows, rows // peers, LANES)
        normed = among_heads(normed.swapaxes(1, 2).reshape(heads, rows, LANES))
        normed = jnp.stack([normed[step] for step in steps])
        normed = [normed[0:1], normed[1:2], *(normed[i : i + 2] for i in range(2, heads, 2))]
        grads = grads.reshape(16, 3, chunks, 16, LANES).transpose(1, 2, 0, 3, 4)
        grads = grads.reshape(3, chunks, peers, per, LANES).transpose(2, 0, 1, 3, 4)
        grads = grads.reshape(peers, 3 * per_seg, LANES)
    grad_projected = unpack(exchange(grads), rows, heads, segments)
    grad_weight = grad_weight_of(normed, turned, heads, mine)
    return (grad_projected, grad_weight)


def solution(mesh):
    placed = (
        P(("groups", "seq"), None),
        P(("groups", "seq"), None),
        P(("groups", "seq")),
        P(("groups", "seq")),
        P(("groups", "seq")),
        P(("groups", "seq"), None),
        P(),
    )
    return jax.shard_map(
        shards,
        mesh=mesh,
        in_specs=placed,
        out_specs=(P(("groups", "seq"), None), P(("groups", "seq"), None)),
        check_vma=False,
    )
```

```python
import functools

import jax
import jax.numpy as jnp
from jax import lax
from jax.experimental import pallas as pl
from jax.experimental.pallas import tpu as pltpu
from jax.sharding import PartitionSpec as P

norm_eps = 1e-06
LANES = 128
CHUNK = 256
META = 8
bf16 = jnp.bfloat16
f32 = jnp.float32

VMEM = pl.BlockSpec(memory_space=pltpu.VMEM)
SMEM = pl.BlockSpec(memory_space=pltpu.SMEM)
PARAMS = pltpu.CompilerParams(vmem_limit_bytes=24 * 1024 * 1024)
WHOLE = pltpu.CompilerParams(vmem_limit_bytes=60 * 1024 * 1024)
ANY = pl.BlockSpec(memory_space=pl.ANY)


def dot(a, b):
    return lax.dot_general(a, b, (((1,), (0,)), ((), ())), preferred_element_type=f32)


def dot_nt(a, b):
    return lax.dot_general(a, b, (((1,), (1,)), ((), ())), preferred_element_type=f32)


def dot_tn(a, b):
    return lax.dot_general(a, b, (((0,), (0,)), ((), ())), preferred_element_type=f32)


def halves(value):
    high = value.astype(bf16)
    return high, (value - high.astype(f32)).astype(bf16)


def wide(value):
    return jnp.concatenate([value] * (CHUNK // LANES), axis=1)


def iota(shape, dim):
    return lax.broadcasted_iota(jnp.int32, shape, dim)


def call(body, outs, ins, flops=0, moved=0, **more):
    return pl.pallas_call(
        body,
        out_shape=outs,
        compiler_params=PARAMS,
        cost_estimate=pl.CostEstimate(flops=flops, bytes_accessed=moved, transcendentals=0),
        **more,
    )(*ins)


def pack_kernel(heads, segments, rows_ref, decay_ref, starts_ref, out_ref, decay, flags, sems):
    per = rows_ref.shape[0] // segments
    inner = heads * LANES
    copies = [
        pltpu.make_async_copy(decay_ref, decay, sems.at[0]),
        pltpu.make_async_copy(starts_ref, flags, sems.at[1]),
    ]
    for segment in range(segments):
        for head in range(heads):
            for part in range(3):
                source = rows_ref.at[
                    pl.ds(segment * per, per), pl.ds(part * inner + head * LANES, LANES)
                ]
                target = out_ref.at[segment * heads + head, pl.ds(part * per, per), :]
                copies.append(pltpu.make_async_copy(source, target, sems.at[len(copies)]))
    for copy in copies:
        copy.start()
    for copy in copies[:2]:
        copy.wait()
    line = iota((META, LANES), 0)
    for head in range(heads):
        meta = decay[...].astype(f32)[head : head + 1, :]
        meta = jnp.where(line == 0, meta, jnp.where(line == 1, flags[...].astype(f32), 0.0))
        for segment in range(segments):
            out_ref[segment * heads + head, 3 * per :, :] = meta.astype(bf16)
    for copy in copies[2:]:
        copy.wait()


def pack(projected, decay_log, starts, heads, segments):
    rows = projected.shape[0]
    per = rows // segments
    peers = heads * segments
    if per % 16 == 0:
        return pl.pallas_call(
            functools.partial(pack_kernel, heads, segments),
            out_shape=jax.ShapeDtypeStruct((peers, 3 * per + META, LANES), bf16),
            in_specs=[ANY] * 3,
            out_specs=VMEM,
            scratch_shapes=[
                pltpu.VMEM((heads, rows), bf16),
                pltpu.VMEM((1, rows), jnp.int32),
                pltpu.SemaphoreType.DMA((3 * peers + 2,)),
            ],
            compiler_params=WHOLE,
        )(projected, decay_log.T, starts.reshape(1, rows))
    body = projected.reshape(segments, per, 3, heads, LANES).transpose(0, 3, 2, 1, 4)
    body = body.reshape(peers, 3 * per, LANES)
    flags = jnp.broadcast_to(starts.astype(bf16)[None, None, :], (heads, 1, rows))
    meta = jnp.concatenate(
        [decay_log.T[:, None, :], flags, jnp.zeros((heads, META - 2, rows), bf16)], axis=1
    )
    meta = jnp.broadcast_to(meta[None], (segments, heads, META, LANES)).reshape(peers, META, LANES)
    return jnp.concatenate([body, meta], axis=1)


def unpack_kernel(heads, segments, in_ref, out_ref):
    per = out_ref.shape[0] // segments
    inner = heads * LANES
    for segment in range(segments):
        for head in range(heads):
            for part in range(3):
                at = part * inner + head * LANES
                out_ref[segment * per : (segment + 1) * per, at : at + LANES] = in_ref[
                    segment * heads + head, part * per : (part + 1) * per, :
                ]


def unpack(arrived, rows, heads, segments):
    per = rows // segments
    if per % 16 == 0:
        return call(
            functools.partial(unpack_kernel, heads, segments),
            jax.ShapeDtypeStruct((rows, 3 * heads * LANES), bf16),
            (arrived,),
            moved=4 * arrived.size,
            in_specs=[VMEM],
            out_specs=VMEM,
        )
    body = arrived.reshape(segments, heads, 3, per, LANES).transpose(0, 3, 2, 1, 4)
    return body.reshape(rows, 3 * heads * LANES)


def turns_of(destination_ref, peers):
    turn = jnp.bitwise_and(destination_ref[...], peers - 1).astype(f32)
    return jnp.broadcast_to(turn, (LANES, LANES)).astype(bf16)


def wrapped(value, peers):
    return jnp.where(value < 0.0, value + peers, jnp.where(value >= peers, value - peers, value))


def places(turns, peers, first, count, rows):
    me = lax.axis_index("seq").astype(f32)
    down = iota((rows, LANES), 0)
    chosen = iota((rows, LANES), 1) == first + down % count
    pick = jnp.where(chosen, 1.0, 0.0).astype(bf16)
    turn = dot_nt(pick, turns) + (down // count).astype(f32) - me
    column = (down % count * peers).astype(f32) + wrapped(turn, peers)
    along = iota((8, rows), 1)
    turn = dot_nt(turns[0:8, :], pick) + (along // count).astype(f32) - me
    line = (along % count * peers).astype(f32) + wrapped(turn, peers)
    return chosen, column, line


def grad_normed_kernel(heads, peers, up_ref, destination_ref, weight_ref, even_ref, odd_ref, turned_ref):
    rows = up_ref.shape[0]
    me = lax.axis_index("seq")
    capacity = rows // peers
    turns = turns_of(destination_ref, peers)
    _, column, _ = places(turns, peers, me * capacity, capacity, rows)
    pick = iota((rows, rows), 1).astype(f32) == column
    turned = dot(jnp.where(pick, 1.0, 0.0).astype(bf16), up_ref[...]).astype(bf16)
    turned_ref[...] = turned
    for step in range(heads):
        head = jnp.bitwise_xor(lax.rem(me, heads), step)
        at = pl.multiple_of(head * LANES, LANES)
        out_ref = odd_ref if step % 2 else even_ref
        out_ref[step // 2] = dot_nt(turned, weight_ref[pl.ds(at, LANES), :])


def grad_normed_of(upstream, destination, out_weight, heads, peers):
    rows, width = upstream.shape
    return call(
        functools.partial(grad_normed_kernel, heads, peers),
        (
            jax.ShapeDtypeStruct((heads // 2, rows, LANES), f32),
            jax.ShapeDtypeStruct((heads // 2, rows, LANES), f32),
            jax.ShapeDtypeStruct((rows, width), bf16),
        ),
        (upstream, destination, out_weight),
        flops=2 * rows * out_weight.size,
        moved=2 * (2 * upstream.size + out_weight.size),
        in_specs=[VMEM] * 3,
        out_specs=[VMEM] * 3,
    )


def grad_weight_of(normed, upstream, heads, mine):
    rows, width = upstream.shape
    total = jax.ShapeDtypeStruct((heads * LANES, width), bf16)
    calls = [normed[:2]] + [[pair] for pair in normed[2:]]
    out = None
    for at, pieces in enumerate(calls):
        count = sum(piece.shape[0] for piece in pieces)

        def body(mine_ref, *refs):
            *piece_refs, up_ref, out_ref = refs[: len(pieces) + 1] + refs[-1:]
            step = pl.program_id(0)
            first = 0
            for piece_ref in piece_refs:
                for i in range(piece_ref.shape[0]):

                    @pl.when(step == first)
                    def _(piece_ref=piece_ref, i=i):
                        out_ref[...] = dot_tn(piece_ref[i], up_ref[...]).astype(bf16)

                    first += 1

        given = [] if out is None else [out]
        out = pl.pallas_call(
            body,
            out_shape=total,
            grid_spec=pltpu.PrefetchScalarGridSpec(
                num_scalar_prefetch=1,
                grid=(count,),
                in_specs=[
                    pl.BlockSpec(piece.shape, lambda i, mine: (0, 0, 0)) for piece in pieces
                ]
                + [pl.BlockSpec((rows, width), lambda i, mine: (0, 0))]
                + [ANY for _ in given],
                out_specs=pl.BlockSpec(
                    (LANES, width),
                    lambda i, mine, at=at: (jnp.bitwise_xor(mine[0], 2 * at + i), 0),
                ),
            ),
            input_output_aliases={len(pieces) + 2: 0} if given else {},
            compiler_params=PARAMS,
            cost_estimate=pl.CostEstimate(
                flops=2 * rows * count * LANES * width,
                bytes_accessed=2 * count * LANES * width,
                transcendentals=0,
            ),
        )(mine.reshape(1), *pieces, upstream, *given)
    return out


def part_rows(ref, part, chunk):
    per = ref.shape[1] // 3
    if ref.shape[1] % 16:
        per = (ref.shape[1] - META) // 3
    at = part * per + chunk * 16
    return ref[:, at : at + 16, :].reshape(CHUNK, LANES)


def plan_kernel(heads, chunks, peers, destination_ref, order_ref, reached_ref, chosen_ref):
    per = CHUNK // peers
    turns = turns_of(destination_ref, peers)
    spot = iota((CHUNK, CHUNK), 1).astype(f32)
    for chunk in range(chunks):
        first = (lax.div(lax.axis_index("seq"), heads) * chunks + chunk) * per
        chosen, column, line = places(turns, peers, first, per, CHUNK)
        column = wide(column)
        order_ref[chunk] = jnp.where(line[0:1, :] <= column, 1.0, 0.0).astype(bf16)
        reached_ref[chunk] = jnp.where(spot <= column, 1.0, 0.0).astype(bf16)
        chosen_ref[chunk] = jnp.where(chosen, 1.0, 0.0).astype(bf16)


def state_kernel(
    heads, chunks, rows_ref, meta_ref, order_ref, reached_ref, chosen_ref,
    last_ref, keep_ref, running_ref, count_ref, leave_ref,
):
    peers = meta_ref.shape[0]
    group = CHUNK // LANES
    first_block = lax.div(lax.axis_index("seq"), heads) * heads
    lines = peers * META
    meta = meta_ref[:, -META:, :].astype(f32).reshape(lines, LANES).astype(bf16)
    row = iota((CHUNK, lines), 0)
    pick = iota((CHUNK, lines), 1) == lax.div(row, CHUNK // peers) * META
    decays = dot(jnp.where(pick, 1.0, 0.0).astype(bf16), meta).astype(bf16)
    ones = jnp.ones((LANES, LANES), bf16)
    state = jnp.zeros((LANES, LANES), f32)
    before = jnp.ones((1, LANES), f32)
    line = iota((8, LANES), 0)
    for chunk in range(chunks):
        decay = dot(decays * chosen_ref[chunk], ones).astype(bf16)
        running = dot(order_ref[chunk], decay)
        flags = [
            meta_ref[first_block + chunk * group + i, -META:, :].astype(f32)[1:2, :]
            for i in range(group)
        ]
        flags = jnp.broadcast_to(jnp.concatenate(flags, axis=1), (LANES, CHUNK)).astype(bf16)
        count = dot_nt(reached_ref[chunk], flags)
        last_run = jnp.min(running, axis=0, keepdims=True)
        last_count = jnp.max(count, axis=0, keepdims=True)
        leave = jnp.exp(jnp.minimum(last_run - running, 0.0))
        leave = jnp.where(count == last_count, leave, 0.0)
        total = jnp.where(last_count == 0.0, jnp.exp(last_run), 0.0)
        key, value = (part_rows(rows_ref, part, chunk) for part in (1, 2))
        high, low = halves(key.astype(f32) * leave)
        keep_ref[chunk, 0:LANES, :] = state
        keep_ref[chunk, LANES:, :] = jnp.where(line == 0, before, total)
        state = total * state + dot_tn(high, value) + dot_tn(low, value)
        before = total * before
        running_ref[chunk] = running
        count_ref[chunk] = count
        leave_ref[chunk] = leave
    last_ref[...] = state.astype(bf16)


def inner_kernel(
    chunks, rows_ref, order_ref, running_ref, count_ref, mix_ref, weights_ref, inner_ref, enter_ref
):
    lane = iota((CHUNK, LANES), 1)
    for chunk in range(chunks):
        running, count = running_ref[chunk], count_ref[chunk]
        turned = jnp.where(lane == 0, running, count).T
        same = (order_ref[chunk].astype(f32) > 0.5) & (wide(count) == turned[1:2, :])
        gap = jnp.minimum(wide(running) - turned[0:1, :], 0.0)
        mix = jnp.where(same, jnp.exp(gap), 0.0)
        query, key, value = (part_rows(rows_ref, part, chunk) for part in range(3))
        weights = (dot_nt(query, key) * mix).astype(bf16)
        mix_ref[chunk] = mix
        weights_ref[chunk] = weights
        inner_ref[chunk] = dot(weights, value)
        enter_ref[chunk] = jnp.where(count == 0.0, jnp.exp(running), 0.0)


def arriving(came_ref, heads, step):
    segment = lax.div(lax.axis_index("seq"), heads)
    last = lax.div(lax.axis_size("seq"), heads) - 1
    end = 0 if step == 1 else last
    return jnp.where(segment == end, 0.0, came_ref[...].astype(f32))


def entering(keep_ref, chunk, came):
    keep = keep_ref[chunk]
    return halves(keep[0:LANES, :] + keep[LANES : LANES + 1, :] * came), keep[LANES + 1 : LANES + 2, :]


def output_kernel(
    heads, chunks, runs, rows_ref, inner_ref, enter_ref, keep_ref, came_ref, *refs
):
    given, (grad_ref, block_ref, back_ref, last_ref, normal_ref, sems) = refs[:-6], refs[-6:]
    mine = lax.rem(lax.axis_index("seq"), heads)
    sources = [given[0].at[0], given[1].at[0]]
    for pair in given[2:]:
        sources += [pair.at[0], pair.at[1]]
    copies = [
        pltpu.make_async_copy(
            source, normal_ref.at[jnp.bitwise_xor(mine, step)], sems.at[step]
        )
        for step, source in enumerate(sources)
    ]
    for copy in copies:
        copy.start()
    group = CHUNK // LANES
    back = jnp.zeros((LANES, LANES), f32)
    after = jnp.ones((1, LANES), f32)
    line = iota((8, LANES), 0)
    came = arriving(came_ref, heads, 1)
    normed_rows = []
    for chunk in range(chunks):
        query = part_rows(rows_ref, 0, chunk)
        enter = enter_ref[chunk]
        (high, low), _ = entering(keep_ref, chunk, came)
        output = inner_ref[chunk] + enter * (dot(query, high) + dot(query, low))
        scale = lax.rsqrt(jnp.mean(output * output, axis=1, keepdims=True) + norm_eps)
        normed = output * scale
        split = normed.reshape(runs, group, CHUNK // (runs * group), LANES)
        for i in range(group):
            step = jnp.bitwise_xor(mine, chunk * group + i)
            at = jnp.bitwise_and(step, 1) * (heads // 2) + lax.div(step, 2)
            block_ref[at] = split[:, i].reshape(LANES, LANES).astype(bf16)
        normed_rows.append((normed, scale))
    for copy in copies:
        copy.wait()
    for chunk in reversed(range(chunks)):
        normed, scale = normed_rows[chunk]
        query = part_rows(rows_ref, 0, chunk)
        enter = enter_ref[chunk]
        normal = jnp.concatenate(
            [
                normal_ref[chunk * group + i].reshape(runs, 1, CHUNK // (runs * group), LANES)
                for i in range(group)
            ],
            axis=1,
        ).reshape(CHUNK, LANES)
        grad = (
            (normal - normed * jnp.mean(normal * normed, axis=1, keepdims=True)) * scale
        ).astype(bf16)
        grad_ref[chunk] = grad
        gain = keep_ref[chunk, LANES + 1 : LANES + 2, :]
        back_ref[chunk, 0:LANES, :] = back
        back_ref[chunk, LANES:, :] = jnp.where(line == 0, after, gain)
        high, low = halves(query.astype(f32) * enter)
        back = gain * back + dot_tn(high, grad) + dot_tn(low, grad)
        after = gain * after
    last_ref[...] = back.astype(bf16)


def local_kernel(
    heads, chunks, rows_ref, mix_ref, weights_ref, enter_ref, keep_ref, came_ref, grad_ref, query_ref, part_ref
):
    came = arriving(came_ref, heads, 1)
    for chunk in range(chunks):
        query, key, value = (part_rows(rows_ref, part, chunk) for part in range(3))
        grad = grad_ref[chunk]
        (high, low), _ = entering(keep_ref, chunk, came)
        grad_mix = (dot_nt(grad, value) * mix_ref[chunk]).astype(bf16)
        grad_query = dot_nt(grad, high) + dot_nt(grad, low)
        grad_query = dot(grad_mix, key) + enter_ref[chunk] * grad_query
        query_ref[:, chunk * 16 : (chunk + 1) * 16, :] = (
            grad_query.astype(bf16).reshape(16, 16, LANES)
        )
        part_ref[0, chunk] = dot_tn(grad_mix, query)
        part_ref[1, chunk] = dot_tn(weights_ref[chunk], grad)


def final_kernel(heads, chunks, rows_ref, leave_ref, query_ref, part_ref, back_ref, came_ref, out_ref):
    per = chunks * 16
    came = arriving(came_ref, heads, -1)
    out_ref[:, 0:per, :] = query_ref[...]
    for chunk in range(chunks):
        key, value = (part_rows(rows_ref, part, chunk) for part in (1, 2))
        leave = leave_ref[chunk]
        (high, low), _ = entering(back_ref, chunk, came)
        grad_key = part_ref[0, chunk] + leave * (dot_nt(value, high) + dot_nt(value, low))
        grad_value = part_ref[1, chunk] + leave * (dot(key, high) + dot(key, low))
        for part, grad in ((1, grad_key), (2, grad_value)):
            at = part * per + chunk * 16
            out_ref[:, at : at + 16, :] = grad.astype(bf16).reshape(16, 16, LANES)


def carried(last, gain, segments, heads, step):
    if segments == 2:
        pairs = [(i, (i + heads) % (2 * heads)) for i in range(2 * heads)]
        return lax.ppermute(last, "seq", pairs)

    def shift(value, by):
        pairs = [
            (s * heads + h, (s + by * step) * heads + h)
            for s in range(segments)
            for h in range(heads)
            if 0 <= s + by * step < segments
        ]
        return lax.ppermute(value, "seq", pairs)

    state = shift(last, 1)
    if segments > 2:
        gain = shift(gain, 1)
        by = 1
        while by < segments - 1:
            state, gain = state + gain[0:1, :] * shift(state, by), gain * shift(gain, by)
            by *= 2
    return state


def shards(projected, decay_log, destination, source, starts, upstream, out_weight):
    rows = projected.shape[0]
    heads = decay_log.shape[1]
    peers = lax.axis_size("seq")
    segments = peers // heads
    per_seg = rows // segments
    chunks = heads * rows // CHUNK
    per = CHUNK // peers
    me = lax.axis_index("seq")
    segment = me // heads
    groups = [[s * heads + h for h in range(heads)] for s in range(segments)]

    def exchange(value):
        return lax.all_to_all(value, "seq", split_axis=0, concat_axis=0, tiled=True)

    def among_heads(value):
        return lax.all_to_all(
            value, "seq", split_axis=0, concat_axis=0, tiled=True, axis_index_groups=groups
        )

    place = destination.reshape(1, rows)
    arrived = exchange(pack(projected, decay_log, starts, heads, segments))
    even, odd, turned = grad_normed_of(upstream, place, out_weight, heads, peers)
    mine = me % heads
    steps = [jnp.bitwise_xor(mine, step) for step in range(heads)]

    def swap(value, step):
        return lax.ppermute(value, "seq", [(i, i ^ step) for i in range(peers)])

    def deal(even, odd):
        other = swap(odd, 1)
        pairs = [
            swap(jnp.stack([even[step], other[step]]), 2 * step) for step in range(1, heads // 2)
        ]
        return [even[0:1], other[0:1], *pairs]

    if per == 16:
        runs = peers
        meta = arrived
        normal = deal(even, odd)
    else:
        runs = 1
        meta = arrived[:, 3 * per_seg :, :]
        arrived = arrived[:, : 3 * per_seg, :].reshape(peers, 3, chunks, per, LANES)
        arrived = arrived.transpose(1, 2, 0, 3, 4).reshape(3, chunks, 16, 16, LANES)
        arrived = arrived.transpose(2, 0, 1, 3, 4).reshape(16, 3 * chunks * 16, LANES)
        normal = jnp.stack([even, odd], axis=1).reshape(heads, rows, LANES)
        normal = among_heads(jnp.stack([normal[step] for step in steps]))
        normal = normal.reshape(chunks, CHUNK // rows, peers, rows // peers, LANES)
        normal = normal.swapaxes(1, 2).reshape(heads, rows, LANES)
        normal = jnp.stack([normal[step] for step in steps])
        normal = [normal[0:1], normal[1:2], *(normal[i : i + 2] for i in range(2, heads, 2))]

    def shape(*dims, dtype=f32):
        return jax.ShapeDtypeStruct(dims, dtype)

    tall = (chunks, CHUNK, LANES)
    square = (chunks, CHUNK, CHUNK)
    states = (chunks, LANES + 8, LANES)
    low = (16, chunks * 16, LANES)
    unit = 2 * chunks * CHUNK * LANES
    order, reached, chosen = call(
        functools.partial(plan_kernel, heads, chunks, peers),
        (shape(*square, dtype=bf16), shape(*square, dtype=bf16), shape(*tall, dtype=bf16)),
        (place,),
        flops=unit * 256,
        moved=4 * chunks * CHUNK * CHUNK,
        in_specs=[VMEM],
        out_specs=[VMEM] * 3,
    )
    last, keep, running, count, leave = call(
        functools.partial(state_kernel, heads, chunks),
        (
            shape(LANES, LANES, dtype=bf16), shape(*states), shape(*tall), shape(*tall),
            shape(*tall),
        ),
        (arrived, meta, order, reached, chosen),
        flops=unit * 512,
        moved=2 * arrived.size,
        in_specs=[VMEM] * 5,
        out_specs=[VMEM] * 5,
    )
    gain = keep[-1, LANES : LANES + 1] * keep[-1, LANES + 1 : LANES + 2]
    gain = jnp.broadcast_to(gain, (8, LANES))
    came = carried(last, gain, segments, heads, 1)
    mix, weights, inner, enter = call(
        functools.partial(inner_kernel, chunks),
        (shape(*square), shape(*square, dtype=bf16), shape(*tall), shape(*tall)),
        (arrived, order, running, count),
        flops=unit * 1024,
        moved=2 * arrived.size + 8 * chunks * CHUNK * CHUNK,
        in_specs=[VMEM] * 4,
        out_specs=[VMEM] * 4,
    )
    grad, normed, back, last = call(
        functools.partial(output_kernel, heads, chunks, runs),
        (
            shape(*tall, dtype=bf16), shape(heads, rows, LANES, dtype=bf16), shape(*states),
            shape(LANES, LANES, dtype=bf16),
        ),
        (arrived, inner, enter, keep, came, *normal),
        flops=unit * 1024,
        moved=2 * arrived.size + 8 * chunks * CHUNK * LANES,
        in_specs=[VMEM] * 5 + [ANY] * len(normal),
        out_specs=[VMEM] * 4,
        scratch_shapes=[
            pltpu.VMEM((heads, rows, LANES), f32),
            pltpu.SemaphoreType.DMA((heads,)),
        ],
    )
    came_back = carried(last, gain, segments, heads, -1)
    grad_query, part = call(
        functools.partial(local_kernel, heads, chunks),
        (shape(*low, dtype=bf16), shape(2, *tall)),
        (arrived, mix, weights, enter, keep, came, grad),
        flops=unit * 1024,
        moved=2 * arrived.size + 8 * chunks * CHUNK * CHUNK,
        in_specs=[VMEM] * 7,
        out_specs=[VMEM] * 2,
    )
    grads = call(
        functools.partial(final_kernel, heads, chunks),
        shape(16, 3 * chunks * 16, LANES, dtype=bf16),
        (arrived, leave, grad_query, part, back, came_back),
        flops=unit * 512,
        moved=4 * arrived.size,
        in_specs=[VMEM] * 6,
        out_specs=VMEM,
    )
    normed, grads = lax.optimization_barrier((normed, grads))
    if per == 16:
        normed = deal(normed[: heads // 2], normed[heads // 2 :])
    else:
        normed = normed.reshape(2, heads // 2, rows, LANES).swapaxes(0, 1)
        normed = normed.reshape(heads, rows, LANES)
        normed = jnp.stack([normed[step] for step in steps])
        normed = normed.reshape(chunks, peers, CHUNK // rows, rows // peers, LANES)
        normed = among_heads(normed.swapaxes(1, 2).reshape(heads, rows, LANES))
        normed = jnp.stack([normed[step] for step in steps])
        normed = [normed[0:1], normed[1:2], *(normed[i : i + 2] for i in range(2, heads, 2))]
        grads = grads.reshape(16, 3, chunks, 16, LANES).transpose(1, 2, 0, 3, 4)
        grads = grads.reshape(3, chunks, peers, per, LANES).transpose(2, 0, 1, 3, 4)
        grads = grads.reshape(peers, 3 * per_seg, LANES)
    grad_projected = unpack(exchange(grads), rows, heads, segments)
    grad_weight = grad_weight_of(normed, turned, heads, mine)
    return (grad_projected, grad_weight)


def solution(mesh):
    placed = (
        P(("groups", "seq"), None),
        P(("groups", "seq"), None),
        P(("groups", "seq")),
        P(("groups", "seq")),
        P(("groups", "seq")),
        P(("groups", "seq"), None),
        P(),
    )
    return jax.shard_map(
        shards,
        mesh=mesh,
        in_specs=placed,
        out_specs=(P(("groups", "seq"), None), P(("groups", "seq"), None)),
        check_vma=False,
    )
```

```python
import functools

import jax
import jax.numpy as jnp
from jax import lax
from jax.experimental import pallas as pl
from jax.experimental.pallas import tpu as pltpu
from jax.sharding import PartitionSpec as P

norm_eps = 1e-06
LANES = 128
CHUNK = 256
META = 8
bf16 = jnp.bfloat16
f32 = jnp.float32

VMEM = pl.BlockSpec(memory_space=pltpu.VMEM)
SMEM = pl.BlockSpec(memory_space=pltpu.SMEM)
PARAMS = pltpu.CompilerParams(vmem_limit_bytes=24 * 1024 * 1024)
WHOLE = pltpu.CompilerParams(vmem_limit_bytes=60 * 1024 * 1024)
ANY = pl.BlockSpec(memory_space=pl.ANY)


def dot(a, b):
    return lax.dot_general(a, b, (((1,), (0,)), ((), ())), preferred_element_type=f32)


def dot_nt(a, b):
    return lax.dot_general(a, b, (((1,), (1,)), ((), ())), preferred_element_type=f32)


def dot_tn(a, b):
    return lax.dot_general(a, b, (((0,), (0,)), ((), ())), preferred_element_type=f32)


def halves(value):
    high = value.astype(bf16)
    return high, (value - high.astype(f32)).astype(bf16)


def folded(value):
    return value[:, :LANES] + value[:, LANES:]


def wide(value):
    return jnp.concatenate([value] * (CHUNK // LANES), axis=1)


def iota(shape, dim):
    return lax.broadcasted_iota(jnp.int32, shape, dim)


def call(body, outs, ins, flops=0, moved=0, **more):
    return pl.pallas_call(
        body,
        out_shape=outs,
        compiler_params=PARAMS,
        cost_estimate=pl.CostEstimate(flops=flops, bytes_accessed=moved, transcendentals=0),
        **more,
    )(*ins)


def pack_kernel(
    heads, segments, rows_ref, decay_ref, starts_ref, out_ref, held, stage, decay, flags, sems, out_sems
):
    per = rows_ref.shape[0] // segments
    inner = heads * LANES
    quarter = per // 2
    arriving = [
        pltpu.make_async_copy(decay_ref, decay, sems.at[0]),
        pltpu.make_async_copy(starts_ref, flags, sems.at[1]),
    ]
    for i in range(2 * segments):
        here = pl.ds(i * quarter, quarter)
        arriving.append(pltpu.make_async_copy(rows_ref.at[here, :], held.at[here, :], sems.at[2 + i]))
    for copy in arriving:
        copy.start()
    for copy in arriving[:2]:
        copy.wait()
    line = iota((META, LANES), 0)
    leaving = []
    for segment in range(segments):
        for copy in arriving[2 + 2 * segment : 4 + 2 * segment]:
            copy.wait()
        for head in range(heads):
            to = segment * heads + head
            for part in range(3):
                at = part * inner + head * LANES
                stage[to, part * per : (part + 1) * per, :] = held[
                    segment * per : (segment + 1) * per, at : at + LANES
                ]
            meta = decay[...].astype(f32)[head : head + 1, :]
            meta = jnp.where(line == 0, meta, jnp.where(line == 1, flags[...].astype(f32), 0.0))
            stage[to, 3 * per :, :] = meta.astype(bf16)
            leaving.append(pltpu.make_async_copy(stage.at[to], out_ref.at[to], out_sems.at[to]))
            leaving[-1].start()
    for copy in leaving:
        copy.wait()


def pack(projected, decay_log, starts, heads, segments):
    rows = projected.shape[0]
    per = rows // segments
    peers = heads * segments
    if per % 32 == 0:
        return pl.pallas_call(
            functools.partial(pack_kernel, heads, segments),
            out_shape=jax.ShapeDtypeStruct((peers, 3 * per + META, LANES), bf16),
            in_specs=[ANY] * 3,
            out_specs=ANY,
            scratch_shapes=[
                pltpu.VMEM(projected.shape, bf16),
                pltpu.VMEM((peers, 3 * per + META, LANES), bf16),
                pltpu.VMEM((heads, rows), bf16),
                pltpu.VMEM((1, rows), jnp.int32),
                pltpu.SemaphoreType.DMA((2 + 2 * segments,)),
                pltpu.SemaphoreType.DMA((peers,)),
            ],
            compiler_params=WHOLE,
        )(projected, decay_log.T, starts.reshape(1, rows))
    body = projected.reshape(segments, per, 3, heads, LANES).transpose(0, 3, 2, 1, 4)
    body = body.reshape(peers, 3 * per, LANES)
    flags = jnp.broadcast_to(starts.astype(bf16)[None, None, :], (heads, 1, rows))
    meta = jnp.concatenate(
        [decay_log.T[:, None, :], flags, jnp.zeros((heads, META - 2, rows), bf16)], axis=1
    )
    meta = jnp.broadcast_to(meta[None], (segments, heads, META, LANES)).reshape(peers, META, LANES)
    return jnp.concatenate([body, meta], axis=1)


def unpack_kernel(heads, segments, in_ref, out_ref, stage, sems):
    per = out_ref.shape[0] // segments
    inner = heads * LANES
    quarter = per // 2
    copies = []
    for i in range(2 * segments):
        here = slice(i * quarter, (i + 1) * quarter)
        for head in range(heads):
            for part in range(3):
                at = part * inner + head * LANES
                first = part * per + i % 2 * quarter
                stage[here, at : at + LANES] = in_ref[
                    i // 2 * heads + head, first : first + quarter, :
                ]
        here = pl.ds(i * quarter, quarter)
        copies.append(pltpu.make_async_copy(stage.at[here, :], out_ref.at[here, :], sems.at[i]))
        copies[-1].start()
    for copy in copies:
        copy.wait()


def unpack(arrived, rows, heads, segments):
    per = rows // segments
    if per % 32 == 0:
        return call(
            functools.partial(unpack_kernel, heads, segments),
            jax.ShapeDtypeStruct((rows, 3 * heads * LANES), bf16),
            (arrived,),
            moved=4 * arrived.size,
            in_specs=[VMEM],
            out_specs=ANY,
            scratch_shapes=[
                pltpu.VMEM((rows, 3 * heads * LANES), bf16),
                pltpu.SemaphoreType.DMA((2 * segments,)),
            ],
        )
    body = arrived.reshape(segments, heads, 3, per, LANES).transpose(0, 3, 2, 1, 4)
    return body.reshape(rows, 3 * heads * LANES)


def turns_of(destination_ref, peers):
    turn = jnp.bitwise_and(destination_ref[...], peers - 1).astype(f32)
    return jnp.broadcast_to(turn, (LANES, LANES)).astype(bf16)


def wrapped(value, peers):
    return jnp.where(value < 0.0, value + peers, jnp.where(value >= peers, value - peers, value))


def places(turns, peers, first, count, rows):
    me = lax.axis_index("seq").astype(f32)
    down = iota((rows, LANES), 0)
    chosen = iota((rows, LANES), 1) == first + down % count
    pick = jnp.where(chosen, 1.0, 0.0).astype(bf16)
    turn = dot_nt(pick, turns) + (down // count).astype(f32) - me
    column = (down % count * peers).astype(f32) + wrapped(turn, peers)
    along = iota((8, rows), 1)
    turn = dot_nt(turns[0:8, :], pick) + (along // count).astype(f32) - me
    line = (along % count * peers).astype(f32) + wrapped(turn, peers)
    return chosen, column, line


def grad_normed_kernel(heads, peers, up_ref, destination_ref, weight_ref, even_ref, odd_ref, turned_ref):
    rows = up_ref.shape[0]
    me = lax.axis_index("seq")
    capacity = rows // peers
    turns = turns_of(destination_ref, peers)
    _, column, _ = places(turns, peers, me * capacity, capacity, rows)
    pick = iota((rows, rows), 1).astype(f32) == column
    turned = dot(jnp.where(pick, 1.0, 0.0).astype(bf16), up_ref[...]).astype(bf16)
    turned_ref[...] = turned
    for step in range(heads):
        head = jnp.bitwise_xor(lax.rem(me, heads), step)
        at = pl.multiple_of(head * LANES, LANES)
        out_ref = odd_ref if step % 2 else even_ref
        out_ref[step // 2] = dot_nt(turned, weight_ref[pl.ds(at, LANES), :])


def grad_normed_of(upstream, destination, out_weight, heads, peers):
    rows, width = upstream.shape
    return call(
        functools.partial(grad_normed_kernel, heads, peers),
        (
            jax.ShapeDtypeStruct((heads // 2, rows, LANES), f32),
            jax.ShapeDtypeStruct((heads // 2, rows, LANES), f32),
            jax.ShapeDtypeStruct((rows, width), bf16),
        ),
        (upstream, destination, out_weight),
        flops=2 * rows * out_weight.size,
        moved=2 * (2 * upstream.size + out_weight.size),
        in_specs=[VMEM] * 3,
        out_specs=[VMEM] * 3,
    )


def grad_weight_kernel(heads, at, count, *refs):
    given, up_ref, (out_ref, stage, sems) = refs[:count], refs[count], refs[-3:]
    mine = lax.rem(lax.axis_index("seq"), heads)
    one, other = [ref[i] for ref in given for i in range(ref.shape[0])]
    odd = jnp.bitwise_and(mine, 1) == 1
    left = jnp.concatenate([jnp.where(odd, other, one), jnp.where(odd, one, other)], axis=1)
    first = pl.multiple_of(jnp.bitwise_xor(lax.div(mine, 2), at) * 2 * LANES, 2 * LANES)
    tile = up_ref.shape[1] // sems.shape[0]
    copies = []
    for i in range(sems.shape[0]):
        here = pl.ds(i * tile, tile)
        stage[:, here] = dot_tn(left, up_ref[:, here]).astype(bf16)
        there = out_ref.at[pl.ds(first, 2 * LANES), here]
        copies.append(pltpu.make_async_copy(stage.at[:, here], there, sems.at[i]))
        copies[-1].start()
    for copy in copies:
        copy.wait()


def grad_weight_of(normed, upstream):
    rows, width = upstream.shape
    heads = sum(piece.shape[0] for piece in normed)
    out = []
    for at, pieces in enumerate([normed[:2]] + [[pair] for pair in normed[2:]]):
        count = len(pieces)
        out = [
            call(
                functools.partial(grad_weight_kernel, heads, at, count),
                jax.ShapeDtypeStruct((heads * LANES, width), bf16),
                (*pieces, upstream, *out),
                flops=4 * rows * LANES * width,
                moved=4 * LANES * width,
                in_specs=[VMEM] * (count + 1) + [ANY] * len(out),
                out_specs=ANY,
                input_output_aliases={count + 1: 0} if out else {},
                scratch_shapes=[
                    pltpu.VMEM((2 * LANES, width), bf16),
                    pltpu.SemaphoreType.DMA((4,)),
                ],
            )
        ]
    return out[0]


def part_rows(ref, part, chunk):
    per = ref.shape[1] // 3
    if ref.shape[1] % 16:
        per = (ref.shape[1] - META) // 3
    at = part * per + chunk * 16
    return ref[:, at : at + 16, :].reshape(CHUNK, LANES)


def plan_kernel(heads, chunks, peers, destination_ref, order_ref, reached_ref, chosen_ref):
    per = CHUNK // peers
    turns = turns_of(destination_ref, peers)
    spot = iota((CHUNK, CHUNK), 1).astype(f32)
    for chunk in range(chunks):
        first = (lax.div(lax.axis_index("seq"), heads) * chunks + chunk) * per
        chosen, column, line = places(turns, peers, first, per, CHUNK)
        column = wide(column)
        order_ref[chunk] = jnp.where(line[0:1, :] <= column, 1.0, 0.0).astype(bf16)
        reached_ref[chunk] = jnp.where(spot <= column, 1.0, 0.0).astype(bf16)
        chosen_ref[chunk] = jnp.where(chosen, 1.0, 0.0).astype(bf16)


def state_kernel(
    heads, chunks, rows_ref, meta_ref, order_ref, reached_ref, chosen_ref,
    last_ref, keep_ref, running_ref, count_ref, leave_ref,
):
    peers = meta_ref.shape[0]
    group = CHUNK // LANES
    first_block = lax.div(lax.axis_index("seq"), heads) * heads
    lines = peers * META
    meta = meta_ref[:, -META:, :].astype(f32).reshape(lines, LANES).astype(bf16)
    row = iota((CHUNK, lines), 0)
    pick = iota((CHUNK, lines), 1) == lax.div(row, CHUNK // peers) * META
    decays = dot(jnp.where(pick, 1.0, 0.0).astype(bf16), meta).astype(bf16)
    ones = jnp.ones((LANES, LANES), bf16)
    state = jnp.zeros((LANES, LANES), f32)
    before = jnp.ones((1, LANES), f32)
    line = iota((8, LANES), 0)
    for chunk in range(chunks):
        decay = dot(decays * chosen_ref[chunk], ones).astype(bf16)
        running = dot(order_ref[chunk], decay)
        flags = [
            meta_ref[first_block + chunk * group + i, -META:, :].astype(f32)[1:2, :]
            for i in range(group)
        ]
        flags = jnp.broadcast_to(jnp.concatenate(flags, axis=1), (LANES, CHUNK)).astype(bf16)
        count = dot_nt(reached_ref[chunk], flags)
        last_run = jnp.min(running, axis=0, keepdims=True)
        last_count = jnp.max(count, axis=0, keepdims=True)
        leave = jnp.exp(jnp.minimum(last_run - running, 0.0))
        leave = jnp.where(count == last_count, leave, 0.0)
        total = jnp.where(last_count == 0.0, jnp.exp(last_run), 0.0)
        key, value = (part_rows(rows_ref, part, chunk) for part in (1, 2))
        high, low = halves(key.astype(f32) * leave)
        keep_ref[chunk, 0:LANES, :] = state
        keep_ref[chunk, LANES:, :] = jnp.where(line == 0, before, total)
        local = folded(dot_tn(value, jnp.concatenate([high, low], axis=1)))
        state = total * state + local
        before = total * before
        running_ref[chunk] = running
        count_ref[chunk] = count
        leave_ref[chunk] = leave
    last_ref[...] = state.astype(bf16)


def inner_kernel(
    heads, chunks, runs, rows_ref, order_ref, running_ref, count_ref, keep_ref, *refs
):
    given, (mix_ref, weights_ref, inner_ref, enter_ref, normal_ref, blocks, sems) = refs[:-7], refs[-7:]
    mine = lax.rem(lax.axis_index("seq"), heads)
    sources = [given[0].at[0], given[1].at[0]]
    for pair in given[2:]:
        sources += [pair.at[0], pair.at[1]]
    copies = [
        pltpu.make_async_copy(source, blocks.at[jnp.bitwise_xor(mine, step)], sems.at[step])
        for step, source in enumerate(sources)
    ]
    for copy in copies:
        copy.start()
    group = CHUNK // LANES
    lane = iota((CHUNK, LANES), 1)
    for chunk in range(chunks):
        running, count = running_ref[chunk], count_ref[chunk]
        turned = jnp.where(lane == 0, running, count).T
        same = (order_ref[chunk].astype(f32) > 0.5) & (wide(count) == turned[1:2, :])
        gap = jnp.minimum(wide(running) - turned[0:1, :], 0.0)
        mix = jnp.where(same, jnp.exp(gap), 0.0)
        query, key, value = (part_rows(rows_ref, part, chunk) for part in range(3))
        weights = (dot_nt(query, key) * mix).astype(bf16)
        mix_ref[chunk] = mix
        weights_ref[chunk] = weights
        inner = dot(weights, value)
        enter = jnp.where(count == 0.0, jnp.exp(running), 0.0)
        if chunk:
            state = jnp.concatenate(halves(keep_ref[chunk, 0:LANES, :]), axis=0)
            inner = inner + enter * folded(dot_nt(query, state))
        inner_ref[chunk] = inner
        enter_ref[chunk] = enter
    for copy in copies:
        copy.wait()
    for chunk in range(chunks):
        normal_ref[chunk] = jnp.concatenate(
            [
                blocks[chunk * group + i].reshape(runs, 1, CHUNK // (runs * group), LANES)
                for i in range(group)
            ],
            axis=1,
        ).reshape(CHUNK, LANES)


def arriving(came_ref, heads, step):
    segment = lax.div(lax.axis_index("seq"), heads)
    last = lax.div(lax.axis_size("seq"), heads) - 1
    end = 0 if step == 1 else last
    return jnp.where(segment == end, 0.0, came_ref[...].astype(f32)).astype(bf16)


def output_kernel(
    heads, chunks, rows_ref, inner_ref, enter_ref, keep_ref, normal_ref, came_ref,
    grad_ref, normed_ref, back_ref, last_ref,
):
    back = jnp.zeros((LANES, LANES), f32)
    after = jnp.ones((1, LANES), f32)
    line = iota((8, LANES), 0)
    came = arriving(came_ref, heads, 1)
    for chunk in reversed(range(chunks)):
        query = part_rows(rows_ref, 0, chunk)
        enter = enter_ref[chunk]
        before = keep_ref[chunk, LANES : LANES + 1, :]
        output = inner_ref[chunk] + before * enter * dot_nt(query, came)
        scale = lax.rsqrt(jnp.mean(output * output, axis=1, keepdims=True) + norm_eps)
        normed = output * scale
        normed_ref[chunk] = normed.astype(bf16)
        normal = normal_ref[chunk]
        grad = (
            (normal - normed * jnp.mean(normal * normed, axis=1, keepdims=True)) * scale
        ).astype(bf16)
        grad_ref[chunk] = grad
        gain = keep_ref[chunk, LANES + 1 : LANES + 2, :]
        back_ref[chunk, 0:LANES, :] = back
        back_ref[chunk, LANES:, :] = jnp.where(line == 0, after, gain)
        high, low = halves(query.astype(f32) * enter)
        back = gain * back + folded(dot_tn(grad, jnp.concatenate([high, low], axis=1)))
        after = gain * after
    last_ref[...] = back.astype(bf16)


def local_kernel(
    heads, chunks, runs, rows_ref, mix_ref, weights_ref, enter_ref, leave_ref, keep_ref, back_ref,
    came_ref, grad_ref, normed_ref, out_ref, part_ref, block_ref, query_ref, sems,
):
    mine = lax.rem(lax.axis_index("seq"), heads)
    group = CHUNK // LANES
    copies = []
    came = arriving(came_ref, heads, 1).astype(f32)
    for chunk in range(chunks):
        query, key, value = (part_rows(rows_ref, part, chunk) for part in range(3))
        grad = grad_ref[chunk]
        state = keep_ref[chunk, 0:LANES, :] + keep_ref[chunk, LANES : LANES + 1, :] * came
        state = jnp.concatenate(halves(state), axis=1)
        grad_mix = (dot_nt(grad, value) * mix_ref[chunk]).astype(bf16)
        grad_query = dot(grad_mix, key) + enter_ref[chunk] * folded(dot(grad, state))
        query_ref[:, chunk * 16 : (chunk + 1) * 16, :] = (
            grad_query.astype(bf16).reshape(16, 16, LANES)
        )
        here = pl.ds(chunk * 16, 16)
        copies.append(
            pltpu.make_async_copy(query_ref.at[:, here, :], out_ref.at[:, here, :], sems.at[chunk])
        )
        copies[-1].start()
        split = normed_ref[chunk].astype(f32).reshape(runs, group, CHUNK // (runs * group), LANES)
        for i in range(group):
            step = jnp.bitwise_xor(mine, chunk * group + i)
            at = jnp.bitwise_and(step, 1) * (heads // 2) + lax.div(step, 2)
            block_ref[at] = split[:, i].reshape(LANES, LANES).astype(bf16)
        grad_key = dot_tn(grad_mix, query)
        grad_value = dot_tn(weights_ref[chunk], grad)
        if chunk < chunks - 1:
            high, low = halves(back_ref[chunk, 0:LANES, :])
            leave = leave_ref[chunk]
            across, down = jnp.concatenate([high, low], axis=1), jnp.concatenate([high, low], axis=0)
            grad_key = grad_key + leave * folded(dot(value, across))
            grad_value = grad_value + leave * folded(dot_nt(key, down))
        part_ref[0, chunk] = grad_key
        part_ref[1, chunk] = grad_value
    for copy in copies:
        copy.wait()


def final_kernel(
    heads, chunks, rows_ref, leave_ref, part_ref, back_ref, came_ref, given_ref, out_ref, stage, sems
):
    per = chunks * 16
    came = arriving(came_ref, heads, -1)
    copies = []
    for chunk in range(chunks):
        key, value = (part_rows(rows_ref, part, chunk) for part in (1, 2))
        leave = leave_ref[chunk] * back_ref[chunk, LANES : LANES + 1, :]
        grad_key = part_ref[0, chunk] + leave * dot(value, came)
        grad_value = part_ref[1, chunk] + leave * dot_nt(key, came)
        for part, grad in ((0, grad_key), (1, grad_value)):
            stage[part, chunk] = grad.astype(bf16).reshape(16, 16, LANES)
            there = pl.ds((part + 1) * per + chunk * 16, 16)
            copy = pltpu.make_async_copy(
                stage.at[part, chunk], out_ref.at[:, there, :], sems.at[len(copies)]
            )
            copy.start()
            copies.append(copy)
    for copy in copies:
        copy.wait()


def carried(last, gain, segments, heads, step):
    if segments == 2:
        pairs = [(i, (i + heads) % (2 * heads)) for i in range(2 * heads)]
        return lax.ppermute(last, "seq", pairs)

    def shift(value, by):
        pairs = [
            (s * heads + h, (s + by * step) * heads + h)
            for s in range(segments)
            for h in range(heads)
            if 0 <= s + by * step < segments
        ]
        return lax.ppermute(value, "seq", pairs)

    state = shift(last, 1)
    if segments > 2:
        gain = shift(gain, 1)
        by = 1
        while by < segments - 1:
            state, gain = state + gain[0:1, :] * shift(state, by), gain * shift(gain, by)
            by *= 2
    return state


def shards(projected, decay_log, destination, source, starts, upstream, out_weight):
    rows = projected.shape[0]
    heads = decay_log.shape[1]
    peers = lax.axis_size("seq")
    segments = peers // heads
    per_seg = rows // segments
    chunks = heads * rows // CHUNK
    per = CHUNK // peers
    me = lax.axis_index("seq")
    segment = me // heads
    groups = [[s * heads + h for h in range(heads)] for s in range(segments)]

    def exchange(value):
        return lax.all_to_all(value, "seq", split_axis=0, concat_axis=0, tiled=True)

    def among_heads(value):
        return lax.all_to_all(
            value, "seq", split_axis=0, concat_axis=0, tiled=True, axis_index_groups=groups
        )

    place = destination.reshape(1, rows)
    arrived = exchange(pack(projected, decay_log, starts, heads, segments))
    even, odd, turned = grad_normed_of(upstream, place, out_weight, heads, peers)
    mine = me % heads
    steps = [jnp.bitwise_xor(mine, step) for step in range(heads)]

    def swap(value, step):
        return lax.ppermute(value, "seq", [(i, i ^ step) for i in range(peers)])

    def deal(even, odd):
        other = swap(odd, 1)
        pairs = [
            swap(jnp.stack([even[step], other[step]]), 2 * step) for step in range(1, heads // 2)
        ]
        return [even[0:1], other[0:1], *pairs]

    if per == 16:
        runs = peers
        meta = arrived
        normal = deal(even, odd)
    else:
        runs = 1
        meta = arrived[:, 3 * per_seg :, :]
        arrived = arrived[:, : 3 * per_seg, :].reshape(peers, 3, chunks, per, LANES)
        arrived = arrived.transpose(1, 2, 0, 3, 4).reshape(3, chunks, 16, 16, LANES)
        arrived = arrived.transpose(2, 0, 1, 3, 4).reshape(16, 3 * chunks * 16, LANES)
        normal = jnp.stack([even, odd], axis=1).reshape(heads, rows, LANES)
        normal = among_heads(jnp.stack([normal[step] for step in steps]))
        normal = normal.reshape(chunks, CHUNK // rows, peers, rows // peers, LANES)
        normal = normal.swapaxes(1, 2).reshape(heads, rows, LANES)
        normal = jnp.stack([normal[step] for step in steps])
        normal = [normal[0:1], normal[1:2], *(normal[i : i + 2] for i in range(2, heads, 2))]

    def shape(*dims, dtype=f32):
        return jax.ShapeDtypeStruct(dims, dtype)

    tall = (chunks, CHUNK, LANES)
    square = (chunks, CHUNK, CHUNK)
    states = (chunks, LANES + 8, LANES)
    unit = 2 * chunks * CHUNK * LANES
    order, reached, chosen = call(
        functools.partial(plan_kernel, heads, chunks, peers),
        (shape(*square, dtype=bf16), shape(*square, dtype=bf16), shape(*tall, dtype=bf16)),
        (place,),
        flops=unit * 256,
        moved=4 * chunks * CHUNK * CHUNK,
        in_specs=[VMEM],
        out_specs=[VMEM] * 3,
    )
    last, keep, running, count, leave = call(
        functools.partial(state_kernel, heads, chunks),
        (
            shape(LANES, LANES, dtype=bf16), shape(*states), shape(*tall), shape(*tall),
            shape(*tall),
        ),
        (arrived, meta, order, reached, chosen),
        flops=unit * 512,
        moved=2 * arrived.size,
        in_specs=[VMEM] * 5,
        out_specs=[VMEM] * 5,
    )
    gain = keep[-1, LANES : LANES + 1] * keep[-1, LANES + 1 : LANES + 2]
    gain = jnp.broadcast_to(gain, (8, LANES))
    came = carried(last, gain, segments, heads, 1)
    mix, weights, inner, enter, normal = call(
        functools.partial(inner_kernel, heads, chunks, runs),
        (shape(*square), shape(*square, dtype=bf16), shape(*tall), shape(*tall), shape(*tall)),
        (arrived, order, running, count, keep, *normal),
        flops=unit * 1024,
        moved=2 * arrived.size + 8 * chunks * CHUNK * CHUNK,
        in_specs=[VMEM] * 5 + [ANY] * len(normal),
        out_specs=[VMEM] * 5,
        scratch_shapes=[
            pltpu.VMEM((heads, rows, LANES), f32),
            pltpu.SemaphoreType.DMA((heads,)),
        ],
    )
    grad, normed, back, last = call(
        functools.partial(output_kernel, heads, chunks),
        (
            shape(*tall, dtype=bf16), shape(*tall, dtype=bf16), shape(*states),
            shape(LANES, LANES, dtype=bf16),
        ),
        (arrived, inner, enter, keep, normal, came),
        flops=unit * 1024,
        moved=2 * arrived.size + 8 * chunks * CHUNK * LANES,
        in_specs=[VMEM] * 6,
        out_specs=[VMEM] * 4,
    )
    came_back = carried(last, gain, segments, heads, -1)
    full = shape(16, 3 * chunks * 16, LANES, dtype=bf16)
    grads, part, normed = call(
        functools.partial(local_kernel, heads, chunks, runs),
        (full, shape(2, *tall), shape(heads, rows, LANES, dtype=bf16)),
        (arrived, mix, weights, enter, leave, keep, back, came, grad, normed),
        flops=unit * 1024,
        moved=2 * arrived.size + 8 * chunks * CHUNK * CHUNK,
        in_specs=[VMEM] * 10,
        out_specs=[ANY] + [VMEM] * 2,
        scratch_shapes=[
            pltpu.VMEM((16, chunks * 16, LANES), bf16),
            pltpu.SemaphoreType.DMA((chunks,)),
        ],
    )
    grads = call(
        functools.partial(final_kernel, heads, chunks),
        full,
        (arrived, leave, part, back, came_back, grads),
        flops=unit * 512,
        moved=4 * arrived.size,
        in_specs=[VMEM] * 5 + [ANY],
        out_specs=ANY,
        input_output_aliases={5: 0},
        scratch_shapes=[
            pltpu.VMEM((2, chunks, 16, 16, LANES), bf16),
            pltpu.SemaphoreType.DMA((2 * chunks,)),
        ],
    )
    normed, grads = lax.optimization_barrier((normed, grads))
    if per == 16:
        normed = deal(normed[: heads // 2], normed[heads // 2 :])
    else:
        normed = normed.reshape(2, heads // 2, rows, LANES).swapaxes(0, 1)
        normed = normed.reshape(heads, rows, LANES)
        normed = jnp.stack([normed[step] for step in steps])
        normed = normed.reshape(chunks, peers, CHUNK // rows, rows // peers, LANES)
        normed = among_heads(normed.swapaxes(1, 2).reshape(heads, rows, LANES))
        normed = jnp.stack([normed[step] for step in steps])
        normed = [normed[0:1], normed[1:2], *(normed[i : i + 2] for i in range(2, heads, 2))]
        grads = grads.reshape(16, 3, chunks, 16, LANES).transpose(1, 2, 0, 3, 4)
        grads = grads.reshape(3, chunks, peers, per, LANES).transpose(2, 0, 1, 3, 4)
        grads = grads.reshape(peers, 3 * per_seg, LANES)
    grad_projected = unpack(exchange(grads), rows, heads, segments)
    grad_weight = grad_weight_of(normed, turned)
    return (grad_projected, grad_weight)


def solution(mesh):
    placed = (
        P(("groups", "seq"), None),
        P(("groups", "seq"), None),
        P(("groups", "seq")),
        P(("groups", "seq")),
        P(("groups", "seq")),
        P(("groups", "seq"), None),
        P(),
    )
    return jax.shard_map(
        shards,
        mesh=mesh,
        in_specs=placed,
        out_specs=(P(("groups", "seq"), None), P(("groups", "seq"), None)),
        check_vma=False,
    )
```

```python
import functools

import jax
import jax.numpy as jnp
from jax import lax
from jax.experimental import pallas as pl
from jax.experimental.pallas import tpu as pltpu
from jax.sharding import PartitionSpec as P

norm_eps = 1e-06
LANES = 128
CHUNK = 256
META = 8
bf16 = jnp.bfloat16
f32 = jnp.float32

VMEM = pl.BlockSpec(memory_space=pltpu.VMEM)
SMEM = pl.BlockSpec(memory_space=pltpu.SMEM)
PARAMS = pltpu.CompilerParams(vmem_limit_bytes=24 * 1024 * 1024)
WHOLE = pltpu.CompilerParams(vmem_limit_bytes=60 * 1024 * 1024)
ANY = pl.BlockSpec(memory_space=pl.ANY)


def dot(a, b):
    return lax.dot_general(a, b, (((1,), (0,)), ((), ())), preferred_element_type=f32)


def dot_nt(a, b):
    return lax.dot_general(a, b, (((1,), (1,)), ((), ())), preferred_element_type=f32)


def dot_tn(a, b):
    return lax.dot_general(a, b, (((0,), (0,)), ((), ())), preferred_element_type=f32)


def halves(value):
    high = value.astype(bf16)
    return high, (value - high.astype(f32)).astype(bf16)


def folded(value):
    return value[:, :LANES] + value[:, LANES:]


def wide(value):
    return jnp.concatenate([value] * (CHUNK // LANES), axis=1)


def iota(shape, dim):
    return lax.broadcasted_iota(jnp.int32, shape, dim)


def call(body, outs, ins, flops=0, moved=0, **more):
    return pl.pallas_call(
        body,
        out_shape=outs,
        compiler_params=PARAMS,
        cost_estimate=pl.CostEstimate(flops=flops, bytes_accessed=moved, transcendentals=0),
        **more,
    )(*ins)


def pack_kernel(
    heads, segments, rows_ref, decay_ref, starts_ref, out_ref, held, stage, decay, flags, sems, out_sems
):
    per = rows_ref.shape[0] // segments
    inner = heads * LANES
    peers = heads * segments
    quarter = per // 2
    arriving = [
        pltpu.make_async_copy(decay_ref, decay, sems.at[0]),
        pltpu.make_async_copy(starts_ref, flags, sems.at[1]),
    ]
    for i in range(2 * segments):
        here = pl.ds(i * quarter, quarter)
        arriving.append(pltpu.make_async_copy(rows_ref.at[here, :], held.at[here, :], sems.at[2 + i]))
    for copy in arriving:
        copy.start()
    for copy in arriving[:2]:
        copy.wait()
    chunks = heads * rows_ref.shape[0] // CHUNK
    spots = CHUNK // peers
    first = lax.rem(lax.axis_index("seq") * spots, LANES)
    line = iota((META, LANES), 0)
    row, spot = iota((LANES, LANES), 0), iota((LANES, LANES), 1) - first
    placed = []
    for i in range(segments * chunks):
        pick = (spot >= 0) & (spot < spots) & (row == i * spots + spot)
        placed.append(dot(decay[...], jnp.where(pick, 1.0, 0.0).astype(bf16)))
    leaving = []
    for segment in range(segments):
        for copy in arriving[2 + 2 * segment : 4 + 2 * segment]:
            copy.wait()
        for head in range(heads):
            to = segment * heads + head
            for part in range(3):
                at = part * inner + head * LANES
                stage[to, part * per : (part + 1) * per, :] = held[
                    segment * per : (segment + 1) * per, at : at + LANES
                ]
            meta = jnp.where(line == chunks, flags[...].astype(f32), 0.0)
            for i in range(chunks):
                here = placed[segment * chunks + i][head : head + 1, :]
                meta = jnp.where(line == i, here, meta)
            stage[to, 3 * per :, :] = meta.astype(bf16)
            leaving.append(pltpu.make_async_copy(stage.at[to], out_ref.at[to], out_sems.at[to]))
            leaving[-1].start()
    for copy in leaving:
        copy.wait()


def pack(projected, decay_log, starts, heads, segments):
    rows = projected.shape[0]
    per = rows // segments
    peers = heads * segments
    if per % 32 == 0:
        return pl.pallas_call(
            functools.partial(pack_kernel, heads, segments),
            out_shape=jax.ShapeDtypeStruct((peers, 3 * per + META, LANES), bf16),
            in_specs=[ANY] * 3,
            out_specs=ANY,
            scratch_shapes=[
                pltpu.VMEM(projected.shape, bf16),
                pltpu.VMEM((peers, 3 * per + META, LANES), bf16),
                pltpu.VMEM((heads, rows), bf16),
                pltpu.VMEM((1, rows), jnp.int32),
                pltpu.SemaphoreType.DMA((2 + 2 * segments,)),
                pltpu.SemaphoreType.DMA((peers,)),
            ],
            compiler_params=WHOLE,
        )(projected, decay_log.T, starts.reshape(1, rows))
    body = projected.reshape(segments, per, 3, heads, LANES).transpose(0, 3, 2, 1, 4)
    body = body.reshape(peers, 3 * per, LANES)
    chunks = heads * rows // CHUNK
    spots = CHUNK // peers
    first = lax.axis_index("seq") * spots % LANES
    decays = decay_log.T.reshape(heads, segments, chunks, spots).swapaxes(0, 1)
    placed = lax.dynamic_update_slice(
        jnp.zeros((segments, heads, chunks, LANES), bf16), decays, (0, 0, 0, first)
    ).reshape(peers, chunks, LANES)
    flags = jnp.broadcast_to(starts.astype(bf16)[None, None, :], (peers, 1, rows))
    blank = jnp.zeros((peers, META - 1 - chunks, LANES), bf16)
    meta = jnp.concatenate([placed, flags, blank], axis=1)
    return jnp.concatenate([body, meta], axis=1)


def unpack_kernel(heads, segments, in_ref, out_ref, stage, sems):
    per = out_ref.shape[0] // segments
    inner = heads * LANES
    quarter = per // 2
    copies = []
    for i in range(2 * segments):
        here = slice(i * quarter, (i + 1) * quarter)
        for head in range(heads):
            for part in range(3):
                at = part * inner + head * LANES
                first = part * per + i % 2 * quarter
                stage[here, at : at + LANES] = in_ref[
                    i // 2 * heads + head, first : first + quarter, :
                ]
        here = pl.ds(i * quarter, quarter)
        copies.append(pltpu.make_async_copy(stage.at[here, :], out_ref.at[here, :], sems.at[i]))
        copies[-1].start()
    for copy in copies:
        copy.wait()


def unpack(arrived, rows, heads, segments):
    per = rows // segments
    if per % 32 == 0:
        return call(
            functools.partial(unpack_kernel, heads, segments),
            jax.ShapeDtypeStruct((rows, 3 * heads * LANES), bf16),
            (arrived,),
            moved=4 * arrived.size,
            in_specs=[VMEM],
            out_specs=ANY,
            scratch_shapes=[
                pltpu.VMEM((rows, 3 * heads * LANES), bf16),
                pltpu.SemaphoreType.DMA((2 * segments,)),
            ],
        )
    body = arrived.reshape(segments, heads, 3, per, LANES).transpose(0, 3, 2, 1, 4)
    return body.reshape(rows, 3 * heads * LANES)


def turns_of(destination_ref, peers):
    turn = jnp.bitwise_and(destination_ref[...], peers - 1).astype(f32)
    return jnp.broadcast_to(turn, (LANES, LANES)).astype(bf16)


def wrapped(value, peers):
    return jnp.where(value < 0.0, value + peers, jnp.where(value >= peers, value - peers, value))


def places(turns, peers, first, count, rows):
    me = lax.axis_index("seq").astype(f32)
    down = iota((rows, LANES), 0)
    chosen = iota((rows, LANES), 1) == first + down % count
    pick = jnp.where(chosen, 1.0, 0.0).astype(bf16)
    turn = dot_nt(pick, turns) + (down // count).astype(f32) - me
    column = (down % count * peers).astype(f32) + wrapped(turn, peers)
    along = iota((8, rows), 1)
    turn = dot_nt(turns[0:8, :], pick) + (along // count).astype(f32) - me
    line = (along % count * peers).astype(f32) + wrapped(turn, peers)
    return column, line


def grad_normed_kernel(heads, peers, up_ref, destination_ref, weight_ref, even_ref, odd_ref, turned_ref):
    rows = up_ref.shape[0]
    me = lax.axis_index("seq")
    capacity = rows // peers
    turns = turns_of(destination_ref, peers)
    column, _ = places(turns, peers, me * capacity, capacity, rows)
    pick = iota((rows, rows), 1).astype(f32) == column
    turned = dot(jnp.where(pick, 1.0, 0.0).astype(bf16), up_ref[...]).astype(bf16)
    turned_ref[...] = turned
    for step in range(heads):
        head = jnp.bitwise_xor(lax.rem(me, heads), step)
        at = pl.multiple_of(head * LANES, LANES)
        out_ref = odd_ref if step % 2 else even_ref
        out_ref[step // 2] = dot_nt(turned, weight_ref[pl.ds(at, LANES), :])


def grad_normed_of(upstream, destination, out_weight, heads, peers):
    rows, width = upstream.shape
    return call(
        functools.partial(grad_normed_kernel, heads, peers),
        (
            jax.ShapeDtypeStruct((heads // 2, rows, LANES), f32),
            jax.ShapeDtypeStruct((heads // 2, rows, LANES), f32),
            jax.ShapeDtypeStruct((rows, width), bf16),
        ),
        (upstream, destination, out_weight),
        flops=2 * rows * out_weight.size,
        moved=2 * (2 * upstream.size + out_weight.size),
        in_specs=[VMEM] * 3,
        out_specs=[VMEM] * 3,
    )


def grad_weight_kernel(heads, at, count, *refs):
    given, up_ref, (out_ref, stage, sems) = refs[:count], refs[count], refs[-3:]
    mine = lax.rem(lax.axis_index("seq"), heads)
    one, other = [ref[i] for ref in given for i in range(ref.shape[0])]
    odd = jnp.bitwise_and(mine, 1) == 1
    left = jnp.concatenate([jnp.where(odd, other, one), jnp.where(odd, one, other)], axis=1)
    first = pl.multiple_of(jnp.bitwise_xor(lax.div(mine, 2), at) * 2 * LANES, 2 * LANES)
    tile = up_ref.shape[1] // sems.shape[0]
    copies = []
    for i in range(sems.shape[0]):
        here = pl.ds(i * tile, tile)
        stage[:, here] = dot_tn(left, up_ref[:, here]).astype(bf16)
        there = out_ref.at[pl.ds(first, 2 * LANES), here]
        copies.append(pltpu.make_async_copy(stage.at[:, here], there, sems.at[i]))
        copies[-1].start()
    for copy in copies:
        copy.wait()


def grad_weight_of(normed, upstream):
    rows, width = upstream.shape
    heads = sum(piece.shape[0] for piece in normed)
    out = []
    pairs = len(normed) - 1
    for at in (0, 1, *range(pairs - 1, 1, -1)):
        pieces = [normed[at + 1]] if at else normed[:2]
        count = len(pieces)
        out = [
            call(
                functools.partial(grad_weight_kernel, heads, at, count),
                jax.ShapeDtypeStruct((heads * LANES, width), bf16),
                (*pieces, upstream, *out),
                flops=4 * rows * LANES * width,
                moved=4 * LANES * width,
                in_specs=[VMEM] * (count + 1) + [ANY] * len(out),
                out_specs=ANY,
                input_output_aliases={count + 1: 0} if out else {},
                scratch_shapes=[
                    pltpu.VMEM((2 * LANES, width), bf16),
                    pltpu.SemaphoreType.DMA((4,)),
                ],
            )
        ]
    return out[0]


def part_rows(ref, part, chunk):
    per = ref.shape[1] // 3
    if ref.shape[1] % 16:
        per = (ref.shape[1] - META) // 3
    at = part * per + chunk * 16
    return ref[:, at : at + 16, :].reshape(CHUNK, LANES)


def plan_kernel(heads, chunks, peers, destination_ref, order_ref, reached_ref):
    per = CHUNK // peers
    turns = turns_of(destination_ref, peers)
    spot = iota((CHUNK, CHUNK), 1).astype(f32)
    for chunk in range(chunks):
        first = (lax.div(lax.axis_index("seq"), heads) * chunks + chunk) * per
        column, line = places(turns, peers, first, per, CHUNK)
        column = wide(column)
        order_ref[chunk] = jnp.where(line[0:1, :] <= column, 1.0, 0.0).astype(bf16)
        reached_ref[chunk] = jnp.where(spot <= column, 1.0, 0.0).astype(bf16)


def state_kernel(
    heads, chunks, rows_ref, meta_ref, order_ref, reached_ref,
    last_ref, keep_ref, running_ref, count_ref, leave_ref,
):
    peers = meta_ref.shape[0]
    group = CHUNK // LANES
    first_block = lax.div(lax.axis_index("seq"), heads) * heads
    owners = peers // group
    lines = [
        jnp.sum(meta_ref[i * owners : (i + 1) * owners, -META:, :].astype(f32), axis=0)
        for i in range(group)
    ]
    state = jnp.zeros((LANES, LANES), f32)
    before = jnp.ones((1, LANES), f32)
    line = iota((8, LANES), 0)
    for chunk in range(chunks):
        decay = jnp.concatenate([part[chunk : chunk + 1, :] for part in lines], axis=1)
        decay = jnp.broadcast_to(decay, (LANES, CHUNK)).astype(bf16)
        running = dot_nt(order_ref[chunk], decay)
        flags = [
            meta_ref[first_block + chunk * group + i, -META:, :].astype(f32)[chunks : chunks + 1, :]
            for i in range(group)
        ]
        flags = jnp.broadcast_to(jnp.concatenate(flags, axis=1), (LANES, CHUNK)).astype(bf16)
        count = dot_nt(reached_ref[chunk], flags)
        last_run = jnp.min(running, axis=0, keepdims=True)
        last_count = jnp.max(count, axis=0, keepdims=True)
        leave = jnp.exp(jnp.minimum(last_run - running, 0.0))
        leave = jnp.where(count == last_count, leave, 0.0)
        total = jnp.where(last_count == 0.0, jnp.exp(last_run), 0.0)
        key, value = (part_rows(rows_ref, part, chunk) for part in (1, 2))
        high, low = halves(key.astype(f32) * leave)
        keep_ref[chunk, 0:LANES, :] = state
        keep_ref[chunk, LANES:, :] = jnp.where(line == 0, before, total)
        local = folded(dot_tn(value, jnp.concatenate([high, low], axis=1)))
        state = total * state + local
        before = total * before
        running_ref[chunk] = running
        count_ref[chunk] = count
        leave_ref[chunk] = leave
    last_ref[...] = state.astype(bf16)


def inner_kernel(
    heads, chunks, runs, rows_ref, order_ref, running_ref, count_ref, keep_ref, *refs
):
    given, (mix_ref, weights_ref, inner_ref, enter_ref, normal_ref, sems) = refs[:-6], refs[-6:]
    mine = lax.rem(lax.axis_index("seq"), heads)
    sources = [given[0].at[0], given[1].at[0]]
    for pair in given[2:]:
        sources += [pair.at[0], pair.at[1]]
    group = CHUNK // LANES
    lines = LANES // runs
    copies = []
    for step, source in enumerate(sources):
        block = jnp.bitwise_xor(mine, step)
        here = pl.ds(pl.multiple_of(lax.rem(block, group) * lines, lines), lines)
        target = normal_ref.at[lax.div(block, group), :, here, :]
        copies.append(pltpu.make_async_copy(source, target, sems.at[step]))
        copies[-1].start()
    lane = iota((CHUNK, LANES), 1)
    for chunk in range(chunks):
        running, count = running_ref[chunk], count_ref[chunk]
        turned = jnp.where(lane == 0, running, count).T
        same = (order_ref[chunk].astype(f32) > 0.5) & (wide(count) == turned[1:2, :])
        gap = jnp.minimum(wide(running) - turned[0:1, :], 0.0)
        mix = jnp.where(same, jnp.exp(gap), 0.0)
        query, key, value = (part_rows(rows_ref, part, chunk) for part in range(3))
        weights = (dot_nt(query, key) * mix).astype(bf16)
        mix_ref[chunk] = mix
        weights_ref[chunk] = weights
        inner = dot(weights, value)
        enter = jnp.where(count == 0.0, jnp.exp(running), 0.0)
        if chunk:
            state = jnp.concatenate(halves(keep_ref[chunk, 0:LANES, :]), axis=0)
            inner = inner + enter * folded(dot_nt(query, state))
        inner_ref[chunk] = inner
        enter_ref[chunk] = enter
    for copy in copies:
        copy.wait()


def arriving(came_ref, heads, step):
    segment = lax.div(lax.axis_index("seq"), heads)
    last = lax.div(lax.axis_size("seq"), heads) - 1
    end = 0 if step == 1 else last
    return jnp.where(segment == end, 0.0, came_ref[...].astype(f32)).astype(bf16)


def output_kernel(
    heads, chunks, rows_ref, inner_ref, enter_ref, keep_ref, normal_ref, came_ref,
    grad_ref, normed_ref, back_ref, last_ref,
):
    back = jnp.zeros((LANES, LANES), f32)
    after = jnp.ones((1, LANES), f32)
    line = iota((8, LANES), 0)
    came = arriving(came_ref, heads, 1)
    for chunk in reversed(range(chunks)):
        query = part_rows(rows_ref, 0, chunk)
        enter = enter_ref[chunk]
        before = keep_ref[chunk, LANES : LANES + 1, :]
        output = inner_ref[chunk] + before * enter * dot_nt(query, came)
        scale = lax.rsqrt(jnp.mean(output * output, axis=1, keepdims=True) + norm_eps)
        normed = output * scale
        normed_ref[chunk] = normed.astype(bf16)
        normal = normal_ref[chunk].reshape(CHUNK, LANES)
        grad = (
            (normal - normed * jnp.mean(normal * normed, axis=1, keepdims=True)) * scale
        ).astype(bf16)
        grad_ref[chunk] = grad
        gain = keep_ref[chunk, LANES + 1 : LANES + 2, :]
        back_ref[chunk, 0:LANES, :] = back
        back_ref[chunk, LANES:, :] = jnp.where(line == 0, after, gain)
        high, low = halves(query.astype(f32) * enter)
        back = gain * back + folded(dot_tn(grad, jnp.concatenate([high, low], axis=1)))
        after = gain * after
    last_ref[...] = back.astype(bf16)


def local_kernel(
    heads, chunks, rows_ref, mix_ref, weights_ref, enter_ref, leave_ref, keep_ref, back_ref,
    came_ref, grad_ref, out_ref, part_ref, query_ref, sems,
):
    copies = []
    came = arriving(came_ref, heads, 1).astype(f32)
    for chunk in range(chunks):
        query, key, value = (part_rows(rows_ref, part, chunk) for part in range(3))
        grad = grad_ref[chunk]
        state = keep_ref[chunk, 0:LANES, :] + keep_ref[chunk, LANES : LANES + 1, :] * came
        state = jnp.concatenate(halves(state), axis=1)
        grad_mix = (dot_nt(grad, value) * mix_ref[chunk]).astype(bf16)
        grad_query = dot(grad_mix, key) + enter_ref[chunk] * folded(dot(grad, state))
        query_ref[:, chunk * 16 : (chunk + 1) * 16, :] = (
            grad_query.astype(bf16).reshape(16, 16, LANES)
        )
        here = pl.ds(chunk * 16, 16)
        copies.append(
            pltpu.make_async_copy(query_ref.at[:, here, :], out_ref.at[:, here, :], sems.at[chunk])
        )
        copies[-1].start()
        grad_key = dot_tn(grad_mix, query)
        grad_value = dot_tn(weights_ref[chunk], grad)
        if chunk < chunks - 1:
            high, low = halves(back_ref[chunk, 0:LANES, :])
            leave = leave_ref[chunk]
            across, down = jnp.concatenate([high, low], axis=1), jnp.concatenate([high, low], axis=0)
            grad_key = grad_key + leave * folded(dot(value, across))
            grad_value = grad_value + leave * folded(dot_nt(key, down))
        part_ref[0, chunk] = grad_key
        part_ref[1, chunk] = grad_value
    for copy in copies:
        copy.wait()


def blocks_kernel(heads, runs, normed_ref, block_ref):
    mine = lax.rem(lax.axis_index("seq"), heads)
    group = CHUNK // LANES
    for chunk in range(normed_ref.shape[0]):
        split = normed_ref[chunk].astype(f32).reshape(runs, group, CHUNK // (runs * group), LANES)
        for i in range(group):
            step = jnp.bitwise_xor(mine, chunk * group + i)
            at = jnp.bitwise_and(step, 1) * (heads // 2) + lax.div(step, 2)
            block_ref[at] = split[:, i].reshape(LANES, LANES).astype(bf16)


def final_kernel(
    heads, chunks, rows_ref, leave_ref, part_ref, back_ref, came_ref, given_ref, out_ref, stage, sems
):
    per = chunks * 16
    came = arriving(came_ref, heads, -1)
    copies = []
    for chunk in range(chunks):
        key, value = (part_rows(rows_ref, part, chunk) for part in (1, 2))
        leave = leave_ref[chunk] * back_ref[chunk, LANES : LANES + 1, :]
        grad_key = part_ref[0, chunk] + leave * dot(value, came)
        grad_value = part_ref[1, chunk] + leave * dot_nt(key, came)
        for part, grad in ((0, grad_key), (1, grad_value)):
            stage[part, chunk] = grad.astype(bf16).reshape(16, 16, LANES)
            there = pl.ds((part + 1) * per + chunk * 16, 16)
            copy = pltpu.make_async_copy(
                stage.at[part, chunk], out_ref.at[:, there, :], sems.at[len(copies)]
            )
            copy.start()
            copies.append(copy)
    for copy in copies:
        copy.wait()


def carried(last, gain, segments, heads, step):
    if segments == 2:
        pairs = [(i, (i + heads) % (2 * heads)) for i in range(2 * heads)]
        return lax.ppermute(last, "seq", pairs)

    def shift(value, by):
        pairs = [
            (s * heads + h, (s + by * step) * heads + h)
            for s in range(segments)
            for h in range(heads)
            if 0 <= s + by * step < segments
        ]
        return lax.ppermute(value, "seq", pairs)

    state = shift(last, 1)
    if segments > 2:
        gain = shift(gain, 1)
        by = 1
        while by < segments - 1:
            state, gain = state + gain[0:1, :] * shift(state, by), gain * shift(gain, by)
            by *= 2
    return state


def shards(projected, decay_log, destination, source, starts, upstream, out_weight):
    rows = projected.shape[0]
    heads = decay_log.shape[1]
    peers = lax.axis_size("seq")
    segments = peers // heads
    per_seg = rows // segments
    chunks = heads * rows // CHUNK
    per = CHUNK // peers
    me = lax.axis_index("seq")
    segment = me // heads
    groups = [[s * heads + h for h in range(heads)] for s in range(segments)]

    def exchange(value):
        return lax.all_to_all(value, "seq", split_axis=0, concat_axis=0, tiled=True)

    def among_heads(value):
        return lax.all_to_all(
            value, "seq", split_axis=0, concat_axis=0, tiled=True, axis_index_groups=groups
        )

    place = destination.reshape(1, rows)
    arrived = exchange(pack(projected, decay_log, starts, heads, segments))
    even, odd, turned = grad_normed_of(upstream, place, out_weight, heads, peers)
    mine = me % heads
    steps = [jnp.bitwise_xor(mine, step) for step in range(heads)]

    def swap(value, step):
        return lax.ppermute(value, "seq", [(i, i ^ step) for i in range(peers)])

    def deal(even, odd):
        other = swap(odd, 1)
        pairs = [
            swap(jnp.stack([even[step], other[step]]), 2 * step) for step in range(1, heads // 2)
        ]
        return [even[0:1], other[0:1], *pairs]

    if per == 16:
        runs = peers
        meta = arrived
        normal = deal(even, odd)
    else:
        runs = 1
        meta = arrived[:, 3 * per_seg :, :]
        arrived = arrived[:, : 3 * per_seg, :].reshape(peers, 3, chunks, per, LANES)
        arrived = arrived.transpose(1, 2, 0, 3, 4).reshape(3, chunks, 16, 16, LANES)
        arrived = arrived.transpose(2, 0, 1, 3, 4).reshape(16, 3 * chunks * 16, LANES)
        normal = jnp.stack([even, odd], axis=1).reshape(heads, rows, LANES)
        normal = among_heads(jnp.stack([normal[step] for step in steps]))
        normal = normal.reshape(chunks, CHUNK // rows, peers, rows // peers, LANES)
        normal = normal.swapaxes(1, 2).reshape(heads, rows, LANES)
        normal = jnp.stack([normal[step] for step in steps])
        normal = [normal[0:1], normal[1:2], *(normal[i : i + 2] for i in range(2, heads, 2))]

    def shape(*dims, dtype=f32):
        return jax.ShapeDtypeStruct(dims, dtype)

    tall = (chunks, CHUNK, LANES)
    square = (chunks, CHUNK, CHUNK)
    states = (chunks, LANES + 8, LANES)
    unit = 2 * chunks * CHUNK * LANES
    order, reached = call(
        functools.partial(plan_kernel, heads, chunks, peers),
        (shape(*square, dtype=bf16), shape(*square, dtype=bf16)),
        (place,),
        flops=unit * 256,
        moved=4 * chunks * CHUNK * CHUNK,
        in_specs=[VMEM],
        out_specs=[VMEM] * 2,
    )
    last, keep, running, count, leave = call(
        functools.partial(state_kernel, heads, chunks),
        (
            shape(LANES, LANES, dtype=bf16), shape(*states), shape(*tall), shape(*tall),
            shape(*tall),
        ),
        (arrived, meta, order, reached),
        flops=unit * 512,
        moved=2 * arrived.size,
        in_specs=[VMEM] * 4,
        out_specs=[VMEM] * 5,
    )
    gain = keep[-1, LANES : LANES + 1] * keep[-1, LANES + 1 : LANES + 2]
    gain = jnp.broadcast_to(gain, (8, LANES))
    came = carried(last, gain, segments, heads, 1)
    mix, weights, inner, enter, normal = call(
        functools.partial(inner_kernel, heads, chunks, runs),
        (
            shape(*square), shape(*square, dtype=bf16), shape(*tall), shape(*tall),
            shape(chunks, runs, CHUNK // runs, LANES),
        ),
        (arrived, order, running, count, keep, *(piece.reshape(-1, runs, rows // runs, LANES) for piece in normal)),
        flops=unit * 1024,
        moved=2 * arrived.size + 8 * chunks * CHUNK * CHUNK,
        in_specs=[VMEM] * 5 + [ANY] * len(normal),
        out_specs=[VMEM] * 5,
        scratch_shapes=[pltpu.SemaphoreType.DMA((heads,))],
    )
    grad, normed, back, last = call(
        functools.partial(output_kernel, heads, chunks),
        (
            shape(*tall, dtype=bf16), shape(*tall, dtype=bf16), shape(*states),
            shape(LANES, LANES, dtype=bf16),
        ),
        (arrived, inner, enter, keep, normal, came),
        flops=unit * 1024,
        moved=2 * arrived.size + 8 * chunks * CHUNK * LANES,
        in_specs=[VMEM] * 6,
        out_specs=[VMEM] * 4,
    )
    came_back = carried(last, gain, segments, heads, -1)
    full = shape(16, 3 * chunks * 16, LANES, dtype=bf16)
    grads, part = call(
        functools.partial(local_kernel, heads, chunks),
        (full, shape(2, *tall)),
        (arrived, mix, weights, enter, leave, keep, back, came, grad),
        flops=unit * 1024,
        moved=2 * arrived.size + 8 * chunks * CHUNK * CHUNK,
        in_specs=[VMEM] * 9,
        out_specs=[ANY, VMEM],
        scratch_shapes=[
            pltpu.VMEM((16, chunks * 16, LANES), bf16),
            pltpu.SemaphoreType.DMA((chunks,)),
        ],
    )
    grads = call(
        functools.partial(final_kernel, heads, chunks),
        full,
        (arrived, leave, part, back, came_back, grads),
        flops=unit * 512,
        moved=4 * arrived.size,
        in_specs=[VMEM] * 5 + [ANY],
        out_specs=ANY,
        input_output_aliases={5: 0},
        scratch_shapes=[
            pltpu.VMEM((2, chunks, 16, 16, LANES), bf16),
            pltpu.SemaphoreType.DMA((2 * chunks,)),
        ],
    )
    normed, grads = lax.optimization_barrier((normed, grads))
    normed = call(
        functools.partial(blocks_kernel, heads, runs),
        shape(heads, rows, LANES, dtype=bf16),
        (normed,),
        moved=4 * normed.size,
        in_specs=[VMEM],
        out_specs=VMEM,
    )
    if per == 16:
        normed = deal(normed[: heads // 2], normed[heads // 2 :])
    else:
        normed = normed.reshape(2, heads // 2, rows, LANES).swapaxes(0, 1)
        normed = normed.reshape(heads, rows, LANES)
        normed = jnp.stack([normed[step] for step in steps])
        normed = normed.reshape(chunks, peers, CHUNK // rows, rows // peers, LANES)
        normed = among_heads(normed.swapaxes(1, 2).reshape(heads, rows, LANES))
        normed = jnp.stack([normed[step] for step in steps])
        normed = [normed[0:1], normed[1:2], *(normed[i : i + 2] for i in range(2, heads, 2))]
        grads = grads.reshape(16, 3, chunks, 16, LANES).transpose(1, 2, 0, 3, 4)
        grads = grads.reshape(3, chunks, peers, per, LANES).transpose(2, 0, 1, 3, 4)
        grads = grads.reshape(peers, 3 * per_seg, LANES)
    grad_projected = unpack(exchange(grads), rows, heads, segments)
    grad_weight = grad_weight_of(normed, turned)
    return (grad_projected, grad_weight)


def solution(mesh):
    placed = (
        P(("groups", "seq"), None),
        P(("groups", "seq"), None),
        P(("groups", "seq")),
        P(("groups", "seq")),
        P(("groups", "seq")),
        P(("groups", "seq"), None),
        P(),
    )
    return jax.shard_map(
        shards,
        mesh=mesh,
        in_specs=placed,
        out_specs=(P(("groups", "seq"), None), P(("groups", "seq"), None)),
        check_vma=False,
    )
```

```python
import functools

import jax
import jax.numpy as jnp
from jax import lax
from jax.experimental import pallas as pl
from jax.experimental.pallas import tpu as pltpu
from jax.sharding import PartitionSpec as P

norm_eps = 1e-06
LANES = 128
CHUNK = 256
META = 8
bf16 = jnp.bfloat16
f32 = jnp.float32

VMEM = pl.BlockSpec(memory_space=pltpu.VMEM)
SMEM = pl.BlockSpec(memory_space=pltpu.SMEM)
PARAMS = pltpu.CompilerParams(vmem_limit_bytes=24 * 1024 * 1024)
WHOLE = pltpu.CompilerParams(vmem_limit_bytes=60 * 1024 * 1024)
ANY = pl.BlockSpec(memory_space=pl.ANY)


def dot(a, b):
    return lax.dot_general(a, b, (((1,), (0,)), ((), ())), preferred_element_type=f32)


def dot_nt(a, b):
    return lax.dot_general(a, b, (((1,), (1,)), ((), ())), preferred_element_type=f32)


def dot_tn(a, b):
    return lax.dot_general(a, b, (((0,), (0,)), ((), ())), preferred_element_type=f32)


def halves(value):
    high = value.astype(bf16)
    return high, (value - high.astype(f32)).astype(bf16)


def folded(value):
    return value[:, :LANES] + value[:, LANES:]


def wide(value):
    return jnp.concatenate([value] * (CHUNK // LANES), axis=1)


def iota(shape, dim):
    return lax.broadcasted_iota(jnp.int32, shape, dim)


def call(body, outs, ins, flops=0, moved=0, **more):
    return pl.pallas_call(
        body,
        out_shape=outs,
        compiler_params=PARAMS,
        cost_estimate=pl.CostEstimate(flops=flops, bytes_accessed=moved, transcendentals=0),
        **more,
    )(*ins)


def pack_kernel(
    heads, segments, rows_ref, decay_ref, starts_ref, out_ref, held, stage, decay, flags, sems, out_sems
):
    per = rows_ref.shape[0] // segments
    inner = heads * LANES
    peers = heads * segments
    quarter = per // 2
    arriving = [
        pltpu.make_async_copy(decay_ref, decay, sems.at[0]),
        pltpu.make_async_copy(starts_ref, flags, sems.at[1]),
    ]
    for i in range(2 * segments):
        here = pl.ds(i * quarter, quarter)
        arriving.append(pltpu.make_async_copy(rows_ref.at[here, :], held.at[here, :], sems.at[2 + i]))
    for copy in arriving:
        copy.start()
    for copy in arriving[:2]:
        copy.wait()
    chunks = heads * rows_ref.shape[0] // CHUNK
    spots = CHUNK // peers
    first = lax.rem(lax.axis_index("seq") * spots, LANES)
    line = iota((META, LANES), 0)
    spot = iota((heads, LANES), 1) - first
    mine = (spot >= 0) & (spot < spots)
    placed = []
    for i in range(segments * chunks):
        turn = lax.rem(first + LANES - i * spots, LANES)
        placed.append(jnp.where(mine, pltpu.roll(decay[...].astype(f32), turn, 1), 0.0))
    leaving = []
    for segment in range(segments):
        for copy in arriving[2 + 2 * segment : 4 + 2 * segment]:
            copy.wait()
        for head in range(heads):
            to = segment * heads + head
            for part in range(3):
                at = part * inner + head * LANES
                stage[to, part * per : (part + 1) * per, :] = held[
                    segment * per : (segment + 1) * per, at : at + LANES
                ]
            meta = jnp.where(line == chunks, flags[...].astype(f32), 0.0)
            for i in range(chunks):
                here = placed[segment * chunks + i][head : head + 1, :]
                meta = jnp.where(line == i, here, meta)
            stage[to, 3 * per :, :] = meta.astype(bf16)
            leaving.append(pltpu.make_async_copy(stage.at[to], out_ref.at[to], out_sems.at[to]))
            leaving[-1].start()
    for copy in leaving:
        copy.wait()


def pack(projected, decay_log, starts, heads, segments):
    rows = projected.shape[0]
    per = rows // segments
    peers = heads * segments
    if per % 32 == 0:
        return pl.pallas_call(
            functools.partial(pack_kernel, heads, segments),
            out_shape=jax.ShapeDtypeStruct((peers, 3 * per + META, LANES), bf16),
            in_specs=[ANY] * 3,
            out_specs=ANY,
            scratch_shapes=[
                pltpu.VMEM(projected.shape, bf16),
                pltpu.VMEM((peers, 3 * per + META, LANES), bf16),
                pltpu.VMEM((heads, rows), bf16),
                pltpu.VMEM((1, rows), jnp.int32),
                pltpu.SemaphoreType.DMA((2 + 2 * segments,)),
                pltpu.SemaphoreType.DMA((peers,)),
            ],
            compiler_params=WHOLE,
        )(projected, decay_log.T, starts.reshape(1, rows))
    body = projected.reshape(segments, per, 3, heads, LANES).transpose(0, 3, 2, 1, 4)
    body = body.reshape(peers, 3 * per, LANES)
    chunks = heads * rows // CHUNK
    spots = CHUNK // peers
    first = lax.axis_index("seq") * spots % LANES
    decays = decay_log.T.reshape(heads, segments, chunks, spots).swapaxes(0, 1)
    placed = lax.dynamic_update_slice(
        jnp.zeros((segments, heads, chunks, LANES), bf16), decays, (0, 0, 0, first)
    ).reshape(peers, chunks, LANES)
    flags = jnp.broadcast_to(starts.astype(bf16)[None, None, :], (peers, 1, rows))
    blank = jnp.zeros((peers, META - 1 - chunks, LANES), bf16)
    meta = jnp.concatenate([placed, flags, blank], axis=1)
    return jnp.concatenate([body, meta], axis=1)


def unpack_kernel(heads, segments, in_ref, out_ref, stage, sems):
    per = out_ref.shape[0] // segments
    inner = heads * LANES
    quarter = per // 2
    copies = []
    for i in range(2 * segments):
        here = slice(i * quarter, (i + 1) * quarter)
        for head in range(heads):
            for part in range(3):
                at = part * inner + head * LANES
                first = part * per + i % 2 * quarter
                stage[here, at : at + LANES] = in_ref[
                    i // 2 * heads + head, first : first + quarter, :
                ]
        here = pl.ds(i * quarter, quarter)
        copies.append(pltpu.make_async_copy(stage.at[here, :], out_ref.at[here, :], sems.at[i]))
        copies[-1].start()
    for copy in copies:
        copy.wait()


def unpack(arrived, rows, heads, segments):
    per = rows // segments
    if per % 32 == 0:
        return call(
            functools.partial(unpack_kernel, heads, segments),
            jax.ShapeDtypeStruct((rows, 3 * heads * LANES), bf16),
            (arrived,),
            moved=4 * arrived.size,
            in_specs=[VMEM],
            out_specs=ANY,
            scratch_shapes=[
                pltpu.VMEM((rows, 3 * heads * LANES), bf16),
                pltpu.SemaphoreType.DMA((2 * segments,)),
            ],
        )
    body = arrived.reshape(segments, heads, 3, per, LANES).transpose(0, 3, 2, 1, 4)
    return body.reshape(rows, 3 * heads * LANES)


def turns_of(destination_ref, peers):
    turn = jnp.bitwise_and(destination_ref[...], peers - 1).astype(f32)
    return jnp.broadcast_to(turn, (LANES, LANES)).astype(bf16)


def wrapped(value, peers):
    return jnp.where(value < 0.0, value + peers, jnp.where(value >= peers, value - peers, value))


def places(turns, peers, first, count, rows):
    me = lax.axis_index("seq").astype(f32)
    down = iota((rows, LANES), 0)
    chosen = iota((rows, LANES), 1) == first + down % count
    pick = jnp.where(chosen, 1.0, 0.0).astype(bf16)
    turn = dot_nt(pick, turns) + (down // count).astype(f32) - me
    column = (down % count * peers).astype(f32) + wrapped(turn, peers)
    along = iota((8, rows), 1)
    turn = dot_nt(turns[0:8, :], pick) + (along // count).astype(f32) - me
    line = (along % count * peers).astype(f32) + wrapped(turn, peers)
    return column, line


def grad_normed_kernel(heads, peers, up_ref, destination_ref, weight_ref, even_ref, odd_ref, turned_ref):
    rows = up_ref.shape[0]
    me = lax.axis_index("seq")
    capacity = rows // peers
    turns = turns_of(destination_ref, peers)
    column, _ = places(turns, peers, me * capacity, capacity, rows)
    pick = iota((rows, rows), 1).astype(f32) == column
    turned = dot(jnp.where(pick, 1.0, 0.0).astype(bf16), up_ref[...]).astype(bf16)
    turned_ref[...] = turned
    for step in range(heads):
        head = jnp.bitwise_xor(lax.rem(me, heads), step)
        at = pl.multiple_of(head * LANES, LANES)
        out_ref = odd_ref if step % 2 else even_ref
        out_ref[step // 2] = dot_nt(turned, weight_ref[pl.ds(at, LANES), :])


def grad_normed_of(upstream, destination, out_weight, heads, peers):
    rows, width = upstream.shape
    return call(
        functools.partial(grad_normed_kernel, heads, peers),
        (
            jax.ShapeDtypeStruct((heads // 2, rows, LANES), f32),
            jax.ShapeDtypeStruct((heads // 2, rows, LANES), f32),
            jax.ShapeDtypeStruct((rows, width), bf16),
        ),
        (upstream, destination, out_weight),
        flops=2 * rows * out_weight.size,
        moved=2 * (2 * upstream.size + out_weight.size),
        in_specs=[VMEM] * 3,
        out_specs=[VMEM] * 3,
    )


def grad_weight_kernel(heads, at, count, *refs):
    given, up_ref, (out_ref, stage, sems) = refs[:count], refs[count], refs[-3:]
    mine = lax.rem(lax.axis_index("seq"), heads)
    one, other = [ref[i] for ref in given for i in range(ref.shape[0])]
    odd = jnp.bitwise_and(mine, 1) == 1
    left = jnp.concatenate([jnp.where(odd, other, one), jnp.where(odd, one, other)], axis=1)
    first = pl.multiple_of(jnp.bitwise_xor(lax.div(mine, 2), at) * 2 * LANES, 2 * LANES)
    tile = up_ref.shape[1] // sems.shape[0]
    copies = []
    for i in range(sems.shape[0]):
        here = pl.ds(i * tile, tile)
        stage[:, here] = dot_tn(left, up_ref[:, here]).astype(bf16)
        there = out_ref.at[pl.ds(first, 2 * LANES), here]
        copies.append(pltpu.make_async_copy(stage.at[:, here], there, sems.at[i]))
        copies[-1].start()
    for copy in copies:
        copy.wait()


def grad_weight_of(normed, upstream):
    rows, width = upstream.shape
    heads = sum(piece.shape[0] for piece in normed)
    out = []
    pairs = len(normed) - 1
    for at in (0, 1, *range(pairs - 1, 1, -1)):
        pieces = [normed[at + 1]] if at else normed[:2]
        count = len(pieces)
        out = [
            call(
                functools.partial(grad_weight_kernel, heads, at, count),
                jax.ShapeDtypeStruct((heads * LANES, width), bf16),
                (*pieces, upstream, *out),
                flops=4 * rows * LANES * width,
                moved=4 * LANES * width,
                in_specs=[VMEM] * (count + 1) + [ANY] * len(out),
                out_specs=ANY,
                input_output_aliases={count + 1: 0} if out else {},
                scratch_shapes=[
                    pltpu.VMEM((2 * LANES, width), bf16),
                    pltpu.SemaphoreType.DMA((4,)),
                ],
            )
        ]
    return out[0]


def part_rows(ref, part, chunk):
    per = ref.shape[1] // 3
    if ref.shape[1] % 16:
        per = (ref.shape[1] - META) // 3
    at = part * per + chunk * 16
    return ref[:, at : at + 16, :].reshape(CHUNK, LANES)


def plan_kernel(heads, chunks, peers, destination_ref, order_ref, reached_ref):
    per = CHUNK // peers
    turns = turns_of(destination_ref, peers)
    spot = iota((CHUNK, CHUNK), 1).astype(f32)
    for chunk in range(chunks):
        first = (lax.div(lax.axis_index("seq"), heads) * chunks + chunk) * per
        column, line = places(turns, peers, first, per, CHUNK)
        column = wide(column)
        order_ref[chunk] = jnp.where(line[0:1, :] <= column, 1.0, 0.0).astype(bf16)
        reached_ref[chunk] = jnp.where(spot <= column, 1.0, 0.0).astype(bf16)


def state_kernel(
    heads, chunks, rows_ref, meta_ref, order_ref, reached_ref,
    last_ref, keep_ref, running_ref, count_ref, leave_ref,
):
    peers = meta_ref.shape[0]
    group = CHUNK // LANES
    first_block = lax.div(lax.axis_index("seq"), heads) * heads
    owners = peers // group
    lines = [
        jnp.sum(meta_ref[i * owners : (i + 1) * owners, -META:, :].astype(f32), axis=0)
        for i in range(group)
    ]
    state = jnp.zeros((LANES, LANES), f32)
    before = jnp.ones((1, LANES), f32)
    line = iota((8, LANES), 0)
    for chunk in range(chunks):
        decay = jnp.concatenate([part[chunk : chunk + 1, :] for part in lines], axis=1)
        decay = jnp.broadcast_to(decay, (LANES, CHUNK)).astype(bf16)
        running = dot_nt(order_ref[chunk], decay)
        flags = [
            meta_ref[first_block + chunk * group + i, -META:, :].astype(f32)[chunks : chunks + 1, :]
            for i in range(group)
        ]
        flags = jnp.broadcast_to(jnp.concatenate(flags, axis=1), (LANES, CHUNK)).astype(bf16)
        count = dot_nt(reached_ref[chunk], flags)
        last_run = jnp.min(running, axis=0, keepdims=True)
        last_count = jnp.max(count, axis=0, keepdims=True)
        leave = jnp.exp(jnp.minimum(last_run - running, 0.0))
        leave = jnp.where(count == last_count, leave, 0.0)
        total = jnp.where(last_count == 0.0, jnp.exp(last_run), 0.0)
        key, value = (part_rows(rows_ref, part, chunk) for part in (1, 2))
        high, low = halves(key.astype(f32) * leave)
        keep_ref[chunk, 0:LANES, :] = state
        keep_ref[chunk, LANES:, :] = jnp.where(line == 0, before, total)
        local = folded(dot_tn(value, jnp.concatenate([high, low], axis=1)))
        state = total * state + local
        before = total * before
        running_ref[chunk] = running
        count_ref[chunk] = count
        leave_ref[chunk] = leave
    last_ref[...] = state.astype(bf16)


def inner_kernel(
    heads, chunks, runs, rows_ref, order_ref, running_ref, count_ref, keep_ref, *refs
):
    given, (mix_ref, weights_ref, inner_ref, enter_ref, normal_ref, sems) = refs[:-6], refs[-6:]
    mine = lax.rem(lax.axis_index("seq"), heads)
    sources = [given[0].at[0], given[1].at[0]]
    for pair in given[2:]:
        sources += [pair.at[0], pair.at[1]]
    group = CHUNK // LANES
    lines = LANES // runs
    copies = []
    for step, source in enumerate(sources):
        block = jnp.bitwise_xor(mine, step)
        here = pl.ds(pl.multiple_of(lax.rem(block, group) * lines, lines), lines)
        target = normal_ref.at[lax.div(block, group), :, here, :]
        copies.append(pltpu.make_async_copy(source, target, sems.at[step]))
        copies[-1].start()
    lane = iota((CHUNK, LANES), 1)
    for chunk in range(chunks):
        running, count = running_ref[chunk], count_ref[chunk]
        turned = jnp.where(lane == 0, running, count).T
        same = (order_ref[chunk].astype(f32) > 0.5) & (wide(count) == turned[1:2, :])
        gap = jnp.minimum(wide(running) - turned[0:1, :], 0.0)
        mix = jnp.where(same, jnp.exp(gap), 0.0)
        query, key, value = (part_rows(rows_ref, part, chunk) for part in range(3))
        weights = (dot_nt(query, key) * mix).astype(bf16)
        mix_ref[chunk] = mix
        weights_ref[chunk] = weights
        inner = dot(weights, value)
        enter = jnp.where(count == 0.0, jnp.exp(running), 0.0)
        if chunk:
            state = jnp.concatenate(halves(keep_ref[chunk, 0:LANES, :]), axis=0)
            inner = inner + enter * folded(dot_nt(query, state))
        inner_ref[chunk] = inner
        enter_ref[chunk] = enter
    for copy in copies:
        copy.wait()


def arriving(came_ref, heads, step):
    segment = lax.div(lax.axis_index("seq"), heads)
    last = lax.div(lax.axis_size("seq"), heads) - 1
    end = 0 if step == 1 else last
    return jnp.where(segment == end, 0.0, came_ref[...].astype(f32)).astype(bf16)


def output_kernel(
    heads, chunks, rows_ref, inner_ref, enter_ref, keep_ref, normal_ref, came_ref,
    grad_ref, normed_ref, back_ref, last_ref,
):
    back = jnp.zeros((LANES, LANES), f32)
    after = jnp.ones((1, LANES), f32)
    line = iota((8, LANES), 0)
    came = arriving(came_ref, heads, 1)
    for chunk in reversed(range(chunks)):
        query = part_rows(rows_ref, 0, chunk)
        enter = enter_ref[chunk]
        before = keep_ref[chunk, LANES : LANES + 1, :]
        output = inner_ref[chunk] + before * enter * dot_nt(query, came)
        scale = lax.rsqrt(jnp.mean(output * output, axis=1, keepdims=True) + norm_eps)
        normed = output * scale
        normed_ref[chunk] = normed.astype(bf16)
        normal = normal_ref[chunk].reshape(CHUNK, LANES)
        grad = (
            (normal - normed * jnp.mean(normal * normed, axis=1, keepdims=True)) * scale
        ).astype(bf16)
        grad_ref[chunk] = grad
        gain = keep_ref[chunk, LANES + 1 : LANES + 2, :]
        back_ref[chunk, 0:LANES, :] = back
        back_ref[chunk, LANES:, :] = jnp.where(line == 0, after, gain)
        high, low = halves(query.astype(f32) * enter)
        back = gain * back + folded(dot_tn(grad, jnp.concatenate([high, low], axis=1)))
        after = gain * after
    last_ref[...] = back.astype(bf16)


def local_kernel(
    heads, chunks, rows_ref, mix_ref, weights_ref, enter_ref, leave_ref, keep_ref, back_ref,
    came_ref, grad_ref, out_ref, part_ref, query_ref, sems,
):
    copies = []
    came = arriving(came_ref, heads, 1).astype(f32)
    for chunk in range(chunks):
        query, key, value = (part_rows(rows_ref, part, chunk) for part in range(3))
        grad = grad_ref[chunk]
        state = keep_ref[chunk, 0:LANES, :] + keep_ref[chunk, LANES : LANES + 1, :] * came
        state = jnp.concatenate(halves(state), axis=1)
        grad_mix = (dot_nt(grad, value) * mix_ref[chunk]).astype(bf16)
        grad_query = dot(grad_mix, key) + enter_ref[chunk] * folded(dot(grad, state))
        query_ref[:, chunk * 16 : (chunk + 1) * 16, :] = (
            grad_query.astype(bf16).reshape(16, 16, LANES)
        )
        here = pl.ds(chunk * 16, 16)
        copies.append(
            pltpu.make_async_copy(query_ref.at[:, here, :], out_ref.at[:, here, :], sems.at[chunk])
        )
        copies[-1].start()
        grad_key = dot_tn(grad_mix, query)
        grad_value = dot_tn(weights_ref[chunk], grad)
        if chunk < chunks - 1:
            high, low = halves(back_ref[chunk, 0:LANES, :])
            leave = leave_ref[chunk]
            across, down = jnp.concatenate([high, low], axis=1), jnp.concatenate([high, low], axis=0)
            grad_key = grad_key + leave * folded(dot(value, across))
            grad_value = grad_value + leave * folded(dot_nt(key, down))
        part_ref[0, chunk] = grad_key
        part_ref[1, chunk] = grad_value
    for copy in copies:
        copy.wait()


def blocks_kernel(heads, runs, normed_ref, block_ref):
    mine = lax.rem(lax.axis_index("seq"), heads)
    group = CHUNK // LANES
    for chunk in range(normed_ref.shape[0]):
        split = normed_ref[chunk].astype(f32).reshape(runs, group, CHUNK // (runs * group), LANES)
        for i in range(group):
            step = jnp.bitwise_xor(mine, chunk * group + i)
            at = jnp.bitwise_and(step, 1) * (heads // 2) + lax.div(step, 2)
            block_ref[at] = split[:, i].reshape(LANES, LANES).astype(bf16)


def final_kernel(
    heads, chunks, rows_ref, leave_ref, part_ref, back_ref, came_ref, given_ref, out_ref, stage, sems
):
    per = chunks * 16
    came = arriving(came_ref, heads, -1)
    copies = []
    for chunk in range(chunks):
        key, value = (part_rows(rows_ref, part, chunk) for part in (1, 2))
        leave = leave_ref[chunk] * back_ref[chunk, LANES : LANES + 1, :]
        grad_key = part_ref[0, chunk] + leave * dot(value, came)
        grad_value = part_ref[1, chunk] + leave * dot_nt(key, came)
        for part, grad in ((0, grad_key), (1, grad_value)):
            stage[part, chunk] = grad.astype(bf16).reshape(16, 16, LANES)
            there = pl.ds((part + 1) * per + chunk * 16, 16)
            copy = pltpu.make_async_copy(
                stage.at[part, chunk], out_ref.at[:, there, :], sems.at[len(copies)]
            )
            copy.start()
            copies.append(copy)
    for copy in copies:
        copy.wait()


def carried(last, gain, segments, heads, step):
    if segments == 2:
        pairs = [(i, (i + heads) % (2 * heads)) for i in range(2 * heads)]
        return lax.ppermute(last, "seq", pairs)

    def shift(value, by):
        pairs = [
            (s * heads + h, (s + by * step) * heads + h)
            for s in range(segments)
            for h in range(heads)
            if 0 <= s + by * step < segments
        ]
        return lax.ppermute(value, "seq", pairs)

    state = shift(last, 1)
    if segments > 2:
        gain = shift(gain, 1)
        by = 1
        while by < segments - 1:
            state, gain = state + gain[0:1, :] * shift(state, by), gain * shift(gain, by)
            by *= 2
    return state


def shards(projected, decay_log, destination, source, starts, upstream, out_weight):
    rows = projected.shape[0]
    heads = decay_log.shape[1]
    peers = lax.axis_size("seq")
    segments = peers // heads
    per_seg = rows // segments
    chunks = heads * rows // CHUNK
    per = CHUNK // peers
    me = lax.axis_index("seq")
    segment = me // heads
    groups = [[s * heads + h for h in range(heads)] for s in range(segments)]

    def exchange(value):
        return lax.all_to_all(value, "seq", split_axis=0, concat_axis=0, tiled=True)

    def among_heads(value):
        return lax.all_to_all(
            value, "seq", split_axis=0, concat_axis=0, tiled=True, axis_index_groups=groups
        )

    place = destination.reshape(1, rows)
    arrived = exchange(pack(projected, decay_log, starts, heads, segments))
    even, odd, turned = grad_normed_of(upstream, place, out_weight, heads, peers)
    mine = me % heads
    steps = [jnp.bitwise_xor(mine, step) for step in range(heads)]

    def swap(value, step):
        return lax.ppermute(value, "seq", [(i, i ^ step) for i in range(peers)])

    def deal(even, odd):
        other = swap(odd, 1)
        pairs = [
            swap(jnp.stack([even[step], other[step]]), 2 * step) for step in range(1, heads // 2)
        ]
        return [even[0:1], other[0:1], *pairs]

    if per == 16:
        runs = peers
        meta = arrived
        normal = deal(even, odd)
    else:
        runs = 1
        meta = arrived[:, 3 * per_seg :, :]
        arrived = arrived[:, : 3 * per_seg, :].reshape(peers, 3, chunks, per, LANES)
        arrived = arrived.transpose(1, 2, 0, 3, 4).reshape(3, chunks, 16, 16, LANES)
        arrived = arrived.transpose(2, 0, 1, 3, 4).reshape(16, 3 * chunks * 16, LANES)
        normal = jnp.stack([even, odd], axis=1).reshape(heads, rows, LANES)
        normal = among_heads(jnp.stack([normal[step] for step in steps]))
        normal = normal.reshape(chunks, CHUNK // rows, peers, rows // peers, LANES)
        normal = normal.swapaxes(1, 2).reshape(heads, rows, LANES)
        normal = jnp.stack([normal[step] for step in steps])
        normal = [normal[0:1], normal[1:2], *(normal[i : i + 2] for i in range(2, heads, 2))]

    def shape(*dims, dtype=f32):
        return jax.ShapeDtypeStruct(dims, dtype)

    tall = (chunks, CHUNK, LANES)
    square = (chunks, CHUNK, CHUNK)
    states = (chunks, LANES + 8, LANES)
    unit = 2 * chunks * CHUNK * LANES
    order, reached = call(
        functools.partial(plan_kernel, heads, chunks, peers),
        (shape(*square, dtype=bf16), shape(*square, dtype=bf16)),
        (place,),
        flops=unit * 256,
        moved=4 * chunks * CHUNK * CHUNK,
        in_specs=[VMEM],
        out_specs=[VMEM] * 2,
    )
    last, keep, running, count, leave = call(
        functools.partial(state_kernel, heads, chunks),
        (
            shape(LANES, LANES, dtype=bf16), shape(*states), shape(*tall), shape(*tall),
            shape(*tall),
        ),
        (arrived, meta, order, reached),
        flops=unit * 512,
        moved=2 * arrived.size,
        in_specs=[VMEM] * 4,
        out_specs=[VMEM] * 5,
    )
    gain = keep[-1, LANES : LANES + 1] * keep[-1, LANES + 1 : LANES + 2]
    gain = jnp.broadcast_to(gain, (8, LANES))
    came = carried(last, gain, segments, heads, 1)
    mix, weights, inner, enter, normal = call(
        functools.partial(inner_kernel, heads, chunks, runs),
        (
            shape(*square), shape(*square, dtype=bf16), shape(*tall), shape(*tall),
            shape(chunks, runs, CHUNK // runs, LANES),
        ),
        (arrived, order, running, count, keep, *(piece.reshape(-1, runs, rows // runs, LANES) for piece in normal)),
        flops=unit * 1024,
        moved=2 * arrived.size + 8 * chunks * CHUNK * CHUNK,
        in_specs=[VMEM] * 5 + [ANY] * len(normal),
        out_specs=[VMEM] * 5,
        scratch_shapes=[pltpu.SemaphoreType.DMA((heads,))],
    )
    grad, normed, back, last = call(
        functools.partial(output_kernel, heads, chunks),
        (
            shape(*tall, dtype=bf16), shape(*tall, dtype=bf16), shape(*states),
            shape(LANES, LANES, dtype=bf16),
        ),
        (arrived, inner, enter, keep, normal, came),
        flops=unit * 1024,
        moved=2 * arrived.size + 8 * chunks * CHUNK * LANES,
        in_specs=[VMEM] * 6,
        out_specs=[VMEM] * 4,
    )
    came_back = carried(last, gain, segments, heads, -1)
    full = shape(16, 3 * chunks * 16, LANES, dtype=bf16)
    grads, part = call(
        functools.partial(local_kernel, heads, chunks),
        (full, shape(2, *tall)),
        (arrived, mix, weights, enter, leave, keep, back, came, grad),
        flops=unit * 1024,
        moved=2 * arrived.size + 8 * chunks * CHUNK * CHUNK,
        in_specs=[VMEM] * 9,
        out_specs=[ANY, VMEM],
        scratch_shapes=[
            pltpu.VMEM((16, chunks * 16, LANES), bf16),
            pltpu.SemaphoreType.DMA((chunks,)),
        ],
    )
    grads = call(
        functools.partial(final_kernel, heads, chunks),
        full,
        (arrived, leave, part, back, came_back, grads),
        flops=unit * 512,
        moved=4 * arrived.size,
        in_specs=[VMEM] * 5 + [ANY],
        out_specs=ANY,
        input_output_aliases={5: 0},
        scratch_shapes=[
            pltpu.VMEM((2, chunks, 16, 16, LANES), bf16),
            pltpu.SemaphoreType.DMA((2 * chunks,)),
        ],
    )
    normed = call(
        functools.partial(blocks_kernel, heads, runs),
        shape(heads, rows, LANES, dtype=bf16),
        (normed,),
        moved=4 * normed.size,
        in_specs=[VMEM],
        out_specs=VMEM,
    )
    if per == 16:
        normed = deal(normed[: heads // 2], normed[heads // 2 :])
    else:
        normed = normed.reshape(2, heads // 2, rows, LANES).swapaxes(0, 1)
        normed = normed.reshape(heads, rows, LANES)
        normed = jnp.stack([normed[step] for step in steps])
        normed = normed.reshape(chunks, peers, CHUNK // rows, rows // peers, LANES)
        normed = among_heads(normed.swapaxes(1, 2).reshape(heads, rows, LANES))
        normed = jnp.stack([normed[step] for step in steps])
        normed = [normed[0:1], normed[1:2], *(normed[i : i + 2] for i in range(2, heads, 2))]
        grads = grads.reshape(16, 3, chunks, 16, LANES).transpose(1, 2, 0, 3, 4)
        grads = grads.reshape(3, chunks, peers, per, LANES).transpose(2, 0, 1, 3, 4)
        grads = grads.reshape(peers, 3 * per_seg, LANES)
    grad_projected = unpack(exchange(grads), rows, heads, segments)
    grad_weight = grad_weight_of(normed, turned)
    return (grad_projected, grad_weight)


def solution(mesh):
    placed = (
        P(("groups", "seq"), None),
        P(("groups", "seq"), None),
        P(("groups", "seq")),
        P(("groups", "seq")),
        P(("groups", "seq")),
        P(("groups", "seq"), None),
        P(),
    )
    return jax.shard_map(
        shards,
        mesh=mesh,
        in_specs=placed,
        out_specs=(P(("groups", "seq"), None), P(("groups", "seq"), None)),
        check_vma=False,
    )
```
